512 devices in a mesh: sub: 64 (over y, x, core), grp: 8 (over z).
Axes of the slice: x: 4, y: 8, z: 8, core: 2. Of those that a mesh axis runs over, the one named last changes fastest.
Arguments:
- deflation: bfloat16 [64, 48, 40, 128], P('sub', 'grp'), may hold values from -0.59765625 to 0.59765625
- operator_tiles: bfloat16 [64, 48, 9, 128, 128], P('sub', 'grp'), may hold values from -0.1875 to 0.1875
- tile_columns: int32 [64, 48, 9], P('sub', 'grp'), may hold values from 0 to 95, as said below
- neighbours: int32 [64, 6], P('sub'), may hold values from -1 to 5, as said below
- send_blocks: int32 [64, 6, 8], P('sub'), may hold values from 0 to 47
- row_owner: int32 [64], replicated, may hold values from 0 to 63, each once
Outputs:
- coarse: float32 [64, 40, 280], P('sub', 'grp')
The draws below stay inside these ranges and needn't reach their ends.
Inputs may be any that keep to these rules, and one draw needn't show every extreme that they name: Neighbour ranks list offset slots in increasing order, then -1; the graph is symmetric (j is a neighbour of i exactly when i is one of j), never names a subdomain outside 0 .. 63, offset +1 is always an edge where it exists, and subdomain 64 // 2 has all six neighbours. `tile_columns`: tile 0 of block row b names the subdomain's own block b; a value 48 + r * 8 + n names only a rank r below the subdomain's degree.
All inputs are finite; a program needn't handle non-finite values.
Results may differ from the reference program's by a relative error of at most 0.01.
Values may be sent and summed in bfloat16 or wider, within the bound.
A program may use at most 64 MiB of HBM per device.

```python
import jax
import jax.numpy as jnp
from jax import lax

K = 40
LANE = 128
NT = 9
NSEND = 8
RANKS = 6
BLK = 48
SUBS = 64
SLOTS = 7


def graph_mask(key):
    graph_key = jax.random.fold_in(key, 101)
    raw = jax.random.randint(graph_key, (SUBS, 3), 0, 2)
    raw = raw.at[:, 0].set(1)
    hub = SUBS // 2
    rows = jnp.arange(SUBS)[:, None]
    steps = jnp.arange(3)[None, :] + 1
    forced = (rows == hub) | (rows + steps == hub)
    edges = jnp.where(forced, 1, raw) * (rows + steps < SUBS).astype(jnp.int32)
    backs = []
    for distance in range(3):
        rolled = jnp.roll(edges[:, distance], distance + 1)
        backs.append(rolled * (jnp.arange(SUBS) >= distance + 1).astype(jnp.int32))
    return jnp.concatenate([edges, jnp.stack(backs, axis=1)], axis=1)


def draw_neighbours(key, part):
    mask = graph_mask(key)
    position = jnp.cumsum(mask, axis=1) - 1
    ranks = jnp.arange(RANKS)
    hit = (mask[:, :, None] == 1) & (position[:, :, None] == ranks[None, None, :])
    listed = jnp.sum(jnp.where(hit, jnp.arange(6)[None, :, None], 0), axis=1)
    degree = jnp.sum(mask, axis=1)
    return jnp.where(ranks[None, :] < degree[:, None], listed, -1).astype(jnp.int32)


def draw_tile_columns(key, part):
    degree = jnp.sum(graph_mask(key), axis=1)
    base = jax.random.fold_in(key, 202)
    key_a, key_b, key_c, key_d = jax.random.split(base, 4)
    shape = (SUBS, BLK, NT)
    select = jax.random.randint(key_a, shape, 0, 3)
    local = jax.random.randint(key_b, shape, 0, BLK)
    ranked = jax.random.randint(key_c, shape, 0, 720720) % degree[:, None, None]
    inner = jax.random.randint(key_d, shape, 0, NSEND)
    columns = jnp.where(select < 2, local, BLK + ranked * NSEND + inner)
    diagonal = jnp.broadcast_to(jnp.arange(BLK)[None, :, None], shape)
    columns = jnp.where(jnp.arange(NT)[None, None, :] == 0, diagonal, columns)
    columns = columns.at[SUBS // 2, 0, 1].set(BLK + RANKS * NSEND - 1)
    return columns.astype(jnp.int32)


def with_ends(result, rng, least, high):
    extent = result.shape
    spot = [jax.random.randint(jax.random.fold_in(rng, axis), (), 0, extent[axis]) for axis in range(len(extent))]
    result = result.at[tuple(spot)].set(least)
    longest = extent.index(max(extent))
    spot[longest] = (spot[longest] + 1) % extent[longest]
    return result.at[tuple(spot)].set(high)


def block_levels(key, extent, cuts, smallest, top_value):
    loudness, own = 1.0, jax.random.fold_in(key, 6)
    for dim, blocks in cuts:
        steps = jnp.exp(jax.random.uniform(jax.random.fold_in(own, dim), (blocks,), jnp.float32, smallest / len(cuts), top_value / len(cuts)))
        loudness = loudness * jnp.repeat(steps, extent[dim] // blocks).reshape([-1 if axis == dim else 1 for axis in range(len(extent))])
    return loudness


def gaussian(rng, extent, spread, limit, cuts=(), kind=jnp.bfloat16):
    factor_of = block_levels(rng, extent, cuts, -0.22, 0.18) if cuts else 1.0
    entries = jax.random.normal(rng, extent, jnp.float32) * spread * factor_of
    return jnp.minimum(jnp.maximum(entries, -limit), limit).astype(kind)


def setup_inputs(seed: int = 0) -> dict:
    seeds = jax.random.split(jax.random.key(seed), 7)
    return {
        "deflation": gaussian(seeds[0], (SUBS, BLK, K, LANE), 0.1, 0.59765625, ((0, 64), (1, 8))),
        "operator_tiles": gaussian(seeds[1], (SUBS, BLK, NT, LANE, LANE), (NT * LANE) ** -0.5, 0.1875, ((0, 64), (1, 8))),
        "tile_columns": draw_tile_columns(jax.random.fold_in(seeds[6], 71), 0),
        "neighbours": draw_neighbours(jax.random.fold_in(seeds[6], 71), 0),
        "send_blocks": with_ends(jax.random.randint(seeds[4], (SUBS, RANKS, NSEND), 0, BLK), jax.random.fold_in(seeds[4], 1), 0, BLK - 1).astype(jnp.int32),
        "row_owner": jax.random.permutation(seeds[5], SUBS).astype(jnp.int32),
    }


def one_subdomain(own_panel, own_tiles, own_columns, own_neighbours, own_received):
    ranked = own_received[jnp.clip(own_neighbours, 0, RANKS - 1)]
    ranked = jnp.where((own_neighbours >= 0)[:, None, None, None], ranked, jnp.zeros_like(ranked))
    columns_all = jnp.concatenate([own_panel, ranked.reshape(RANKS * NSEND, K, LANE)], axis=0)
    tile_panels = columns_all[own_columns]
    products = jnp.einsum("btkc,btrc->btkr", tile_panels.astype(jnp.float32), own_tiles.astype(jnp.float32))
    slot_of = jnp.where(own_columns < BLK, 0, 1 + (own_columns - BLK) // NSEND)
    picker = (slot_of[:, :, None] == jnp.arange(SLOTS)[None, None, :]).astype(jnp.float32)
    image_blocks = jnp.einsum("bts,btkr->bskr", picker, products).astype(jnp.bfloat16)
    galerkin = jnp.einsum("bar,bskr->ask", own_panel.astype(jnp.float32), image_blocks.astype(jnp.float32))
    return galerkin.reshape(K, SLOTS * K)


def reference(deflation, operator_tiles, tile_columns, neighbours, send_blocks, row_owner):
    sent = jax.vmap(lambda blocks, lists: blocks[lists])(deflation, send_blocks)
    offsets = jnp.array([1, 2, 3, -1, -2, -3], dtype=jnp.int32)
    source = jnp.arange(SUBS, dtype=jnp.int32)[:, None] + offsets[None, :]
    valid = (source >= 0) & (source < SUBS)
    clipped = jnp.clip(source, 0, SUBS - 1)
    received = sent[clipped, jnp.arange(RANKS, dtype=jnp.int32)[None, :]]
    received = jnp.where(valid[:, :, None, None, None], received, jnp.zeros_like(received))
    rows_all = lax.map(lambda items: one_subdomain(*items), (deflation, operator_tiles, tile_columns, neighbours, received))
    inverse = jnp.zeros((SUBS,), jnp.int32).at[row_owner].set(jnp.arange(SUBS, dtype=jnp.int32))
    return rows_all[inverse]
```

```python
import functools

import jax
import jax.numpy as jnp
from jax import lax
from jax.experimental import pallas as pl
from jax.experimental.pallas import tpu as pltpu
from jax.sharding import PartitionSpec as P

OFFSETS = (1, 2, 3, -1, -2, -3)
ORDER = (2, 5, 1, 4, 0, 3)
SEND_COUNT = 8
MESH = pl.DeviceIdType.MESH


def kernel(
    sizes,
    defl,
    tiles,
    cols,
    neigh,
    lists,
    owner,
    out,
    panel,
    op,
    y_buf,
    z_buf,
    send_buf,
    recv_buf,
    g_buf,
    g_full,
    part_out,
    part_in,
    row_in,
    pick_out,
    pick_in,
    s_cols,
    s_neigh,
    s_lists,
    s_owner,
    load_sem,
    op_sem,
    table_sem,
    ring_send,
    ring_recv,
    margin_send,
    margin_recv,
    part_send,
    part_recv,
    row_send,
    row_recv,
    pick_send,
    pick_recv,
):
    subs, grps, wide, tall, blocks, width, nt = sizes
    lanes = 128
    own_blocks = blocks * grps
    total_cols = own_blocks + 6 * SEND_COUNT
    n_tiles = blocks * nt
    rows = width // grps
    half = grps // 2
    cut = blocks // 2

    i = lax.axis_index("sub")
    g = lax.axis_index("grp")
    row, col = i // wide, i % wide

    def grp_peer(step):
        return lax.rem(g + step + grps, grps)

    op_copies = [
        pltpu.make_async_copy(tiles.at[0, b], op.at[b], op_sem.at[b]) for b in range(blocks)
    ]
    table_copies = [
        pltpu.make_async_copy(cols, s_cols, table_sem.at[0]),
        pltpu.make_async_copy(neigh, s_neigh, table_sem.at[1]),
        pltpu.make_async_copy(lists, s_lists, table_sem.at[2]),
        pltpu.make_async_copy(owner, s_owner, table_sem.at[3]),
    ]
    own_copy = pltpu.make_async_copy(defl.at[0], panel.at[pl.ds(g * blocks, blocks)], load_sem)
    own_copy.start()
    for copy in op_copies + table_copies:
        copy.start()

    barrier = pltpu.get_barrier_semaphore()
    for step in range(1, grps):
        pl.semaphore_signal(barrier, inc=1, device_id=(i, grp_peer(step)), device_id_type=MESH)
    for step in range(1, wide):
        other = row * wide + lax.rem(col + step, wide)
        pl.semaphore_signal(barrier, inc=1, device_id=(other, g), device_id_type=MESH)
    for step in range(1, tall):
        other = lax.rem(row + step, tall) * wide + col
        pl.semaphore_signal(barrier, inc=1, device_id=(other, g), device_id_type=MESH)
    expected = grps + wide + tall - 3
    for off in OFFSETS:
        there = i + off
        valid = (there >= 0) & (there < subs)

        @pl.when(valid)
        def _():
            pl.semaphore_signal(barrier, inc=1, device_id=(there, g), device_id_type=MESH)

        expected = expected + valid.astype(jnp.int32)
    pl.semaphore_wait(barrier, expected)

    def ring(direction, step, piece):
        sign = 1 if direction == 0 else -1
        origin = grp_peer(-sign * step)
        place = panel.at[pl.ds(origin * blocks + piece * cut, cut)]
        source = defl.at[0, pl.ds(piece * cut, cut)] if step == 0 else place
        return pltpu.make_async_remote_copy(
            src_ref=source,
            dst_ref=place,
            send_sem=ring_send.at[direction, step, piece],
            recv_sem=ring_recv.at[direction, step, piece],
            device_id=(i, grp_peer(sign)),
            device_id_type=MESH,
        )

    def arriving(direction, step, piece):
        sign = 1 if direction == 0 else -1
        origin = grp_peer(-sign * (step + 1))
        place = panel.at[pl.ds(origin * blocks + piece * cut, cut)]
        return pltpu.make_async_remote_copy(
            src_ref=place,
            dst_ref=place,
            send_sem=ring_send.at[direction, step, piece],
            recv_sem=ring_recv.at[direction, step, piece],
            device_id=(i, grp_peer(sign)),
            device_id_type=MESH,
        )

    def travels(direction, step, piece):
        return step < half - 1 or (step == half - 1 and piece == direction)

    for piece in range(2):
        for direction in range(2):
            if travels(direction, 0, piece):
                ring(direction, 0, piece).start()

    def ring_step(step):
        for piece in range(2):
            for direction in range(2):
                if travels(direction, step, piece):
                    arriving(direction, step, piece).wait_recv()
                    if step + 1 < half and travels(direction, step + 1, piece):
                        ring(direction, step + 1, piece).start()

    def products(b):
        op_copies[b].wait()
        mine = panel[g * blocks + b]
        for t in range(nt):
            y_buf[pl.ds((b * nt + t) * width, width), :] = jnp.dot(
                mine, op[b, t], preferred_element_type=jnp.float32
            )

    def by_column(first, last, picker):
        for a in range(first, last):
            mine = y_buf[pl.ds(a, n_tiles, stride=width), :].astype(jnp.bfloat16)
            z_buf[pl.ds(a, total_cols, stride=width), :] = jnp.dot(
                picker, mine, preferred_element_type=jnp.float32
            )

    own_copy.wait()
    per_step = -(-blocks // max(1, half - 1))
    done = 0
    for step in range(half - 1):
        for b in range(done, min(blocks, done + per_step)):
            products(b)
        done = min(blocks, done + per_step)
        ring_step(step)
    for b in range(done, blocks):
        products(b)
    for copy in table_copies:
        copy.wait()
    lane_of = lax.broadcasted_iota(jnp.int32, (8, lanes), 1)
    named = jnp.full((8, lanes), -1, jnp.int32)
    for b in range(blocks):
        for t in range(nt):
            named = jnp.where(lane_of == b * nt + t, s_cols[b, 0, t], named)
    moved = named
    for r in range(6):
        low = own_blocks + r * SEND_COUNT
        within = (named >= low) & (named < low + SEND_COUNT)
        moved = moved + jnp.where(within, (s_neigh[0, r] - r) * SEND_COUNT, 0)
    named = jnp.broadcast_to(moved[0:1, :], (total_cols, lanes))
    hits = lax.broadcasted_iota(jnp.int32, (total_cols, lanes), 0) == named
    picker = jnp.where(hits, 1.0, 0.0).astype(jnp.bfloat16)[:, :n_tiles]
    ring_step(half - 1)

    def margin(o):
        there = i - OFFSETS[o]
        return pltpu.make_async_remote_copy(
            src_ref=send_buf.at[o],
            dst_ref=recv_buf.at[o],
            send_sem=margin_send.at[o],
            recv_sem=margin_recv.at[o],
            device_id=(there, g),
            device_id_type=MESH,
        )

    def inside(there):
        return (there >= 0) & (there < subs)

    for o in ORDER:
        for n in range(SEND_COUNT):
            send_buf[o, n] = panel[s_lists[o, 0, n]]

        @pl.when(inside(i - OFFSETS[o]))
        def _():
            margin(o).start()

    by_column(0, width, picker)

    def contract(first, count, blocks_of):
        left = [
            z_buf[pl.ds((first + n) * width, width), :].astype(jnp.bfloat16)
            for n in range(count)
        ]
        return lax.dot_general(
            jnp.concatenate(left, axis=1),
            jnp.concatenate(blocks_of, axis=1),
            (((1,), (1,)), ((), ())),
            preferred_element_type=jnp.float32,
        )

    g_buf[...] = jnp.zeros_like(g_buf)
    part_out[...] = jnp.zeros_like(part_out)
    g_full[...] = jnp.zeros_like(g_full)
    own = jnp.zeros((width, width), jnp.float32)
    for origin in range(grps):
        own = own + contract(origin * blocks, blocks, [panel[origin * blocks + b] for b in range(blocks)])
    g_full[:, pl.ds(0, width)] = own

    chosen = []
    for target in range(tall):
        place = jnp.int32(0)
        for c in range(1, wide):
            place = jnp.where(s_owner[row * wide + c] == target * wide + col, c, place)
        chosen.append(place)
    origin_row = jnp.int32(0)
    for s in range(subs):
        origin_row = jnp.where(s_owner[s] == i, s // wide, origin_row)

    for o in ORDER:

        @pl.when(inside(i + OFFSETS[o]))
        def _():
            margin(o).wait_recv()
            first = own_blocks + o * SEND_COUNT
            g_buf[o] = contract(first, SEND_COUNT, [recv_buf[o, n] for n in range(SEND_COUNT)])

    for r in range(6):
        slot = s_neigh[0, r]
        value = g_buf[jnp.maximum(slot, 0)]
        g_full[:, pl.ds((r + 1) * width, width)] = jnp.where(
            jnp.full((width, width), slot) >= 0, value, 0.0
        )

    spans = -(-7 * width // lanes)
    for other in range(grps):
        for span in range(spans):
            part_out[other, pl.ds(span * rows, rows), :] = g_full[
                pl.ds(other * rows, rows), pl.ds(span * lanes, lanes)
            ]

    def part(step):
        return pltpu.make_async_remote_copy(
            src_ref=part_out.at[grp_peer(step)],
            dst_ref=part_in.at[step],
            send_sem=part_send.at[step],
            recv_sem=part_recv.at[step],
            device_id=(i, grp_peer(step)),
            device_id_type=MESH,
        )

    near_first = sorted(range(1, grps), key=lambda s: -min(s, grps - s))
    for step in near_first:
        part(step).start()
    summed = part_out[g]
    for step in reversed(near_first):
        part(step).wait_recv()
        summed = summed + part_in[step]

    row_in[0] = summed

    def across(step):
        return pltpu.make_async_remote_copy(
            src_ref=row_in.at[0],
            dst_ref=row_in.at[step],
            send_sem=row_send.at[step],
            recv_sem=row_recv.at[step],
            device_id=(row * wide + lax.rem(col + step, wide), g),
            device_id_type=MESH,
        )

    for step in range(1, wide):
        across(step).start()
    for step in range(1, wide):
        across(step).wait_recv()
    for target in range(tall):
        pick_out[target] = row_in[lax.rem(col - chosen[target] + wide, wide)]

    def along(step):
        return pltpu.make_async_remote_copy(
            src_ref=pick_out.at[lax.rem(row + step, tall)],
            dst_ref=pick_in.at[step],
            send_sem=pick_send.at[step],
            recv_sem=pick_recv.at[step],
            device_id=(lax.rem(row + step, tall) * wide + col, g),
            device_id_type=MESH,
        )

    for step in range(1, tall):
        along(step).start()
    pick_in[0] = pick_out[row]
    for step in range(1, tall):
        along(step).wait_recv()
    final = pick_in[lax.rem(row - origin_row + tall, tall)]
    for span in range(spans):
        count = min(lanes, 7 * width - span * lanes)
        out[:, 0, pl.ds(span * lanes, count)] = final[span * rows : (span + 1) * rows, :count]

    for step in range(half):
        for piece in range(2):
            for direction in range(2):
                if travels(direction, step, piece):
                    ring(direction, step, piece).wait_send()
    for o in ORDER:

        @pl.when(inside(i - OFFSETS[o]))
        def _():
            margin(o).wait_send()

    for step in range(1, grps):
        part(step).wait_send()
    for step in range(1, wide):
        across(step).wait_send()
    for step in range(1, tall):
        along(step).wait_send()


def shards(deflation, operator_tiles, tile_columns, neighbours, send_blocks, row_owner):
    subs, grps = lax.axis_size("sub"), lax.axis_size("grp")
    wide = 1 << (subs.bit_length() // 2)
    tall = subs // wide
    _, blocks, width, lanes = deflation.shape
    nt = operator_tiles.shape[2]
    own_blocks = blocks * grps
    total_cols = own_blocks + 6 * SEND_COUNT
    spans = -(-7 * width // lanes)
    rows = width // grps
    packed = -(-spans * rows // 8) * 8
    bf16, f32, i32 = jnp.bfloat16, jnp.float32, jnp.int32
    dma = pltpu.SemaphoreType.DMA
    sizes = (subs, grps, wide, tall, blocks, width, nt)
    result = pl.pallas_call(
        functools.partial(kernel, sizes),
        out_shape=jax.ShapeDtypeStruct((rows, 1, 7 * width), f32),
        in_specs=[pl.BlockSpec(memory_space=pltpu.HBM)] * 6,
        out_specs=pl.BlockSpec(memory_space=pltpu.VMEM),
        scratch_shapes=[
            pltpu.VMEM((own_blocks, width, lanes), bf16),
            pltpu.VMEM((blocks, nt, lanes, lanes), bf16),
            pltpu.VMEM((blocks * nt * width, lanes), f32),
            pltpu.VMEM((total_cols * width, lanes), f32),
            pltpu.VMEM((6, SEND_COUNT, width, lanes), bf16),
            pltpu.VMEM((6, SEND_COUNT, width, lanes), bf16),
            pltpu.VMEM((6, width, width), f32),
            pltpu.VMEM((width, spans * lanes), f32),
            pltpu.VMEM((grps, packed, lanes), f32),
            pltpu.VMEM((grps, packed, lanes), f32),
            pltpu.VMEM((wide, packed, lanes), f32),
            pltpu.VMEM((tall, packed, lanes), f32),
            pltpu.VMEM((tall, packed, lanes), f32),
            pltpu.SMEM((blocks, 1, nt), i32),
            pltpu.SMEM((1, 6), i32),
            pltpu.SMEM((6, 1, SEND_COUNT), i32),
            pltpu.SMEM((subs,), i32),
            dma,
            dma((blocks,)),
            dma((4,)),
            dma((2, grps // 2, 2)),
            dma((2, grps // 2, 2)),
            dma((6,)),
            dma((6,)),
            dma((grps,)),
            dma((grps,)),
            dma((wide,)),
            dma((wide,)),
            dma((tall,)),
            dma((tall,)),
        ],
        compiler_params=pltpu.CompilerParams(
            collective_id=0, has_side_effects=True, vmem_limit_bytes=60 * 2**20
        ),
    )(
        deflation,
        operator_tiles,
        tile_columns.reshape(blocks, 1, nt),
        neighbours,
        send_blocks.reshape(6, 1, SEND_COUNT),
        row_owner,
    )
    return result.reshape(1, rows, 7 * width)


def solution(mesh):
    placed = (
        P("sub", "grp", None, None),
        P("sub", "grp", None, None, None),
        P("sub", "grp", None),
        P("sub", None),
        P("sub", None, None),
        P(),
    )
    return jax.shard_map(
        shards, mesh=mesh, in_specs=placed, out_specs=P("sub", "grp", None), check_vma=False
    )
```

```python
import functools

import jax
import jax.numpy as jnp
from jax import lax
from jax.experimental import pallas as pl
from jax.experimental.pallas import tpu as pltpu
from jax.sharding import PartitionSpec as P

OFFSETS = (1, 2, 3, -1, -2, -3)
ORDER = (2, 5, 1, 4, 0, 3)
SEND_COUNT = 8
MESH = pl.DeviceIdType.MESH


def kernel(
    sizes,
    defl,
    tiles,
    cols,
    neigh,
    lists,
    owner,
    out,
    mine,
    split,
    half_panel,
    spread,
    op,
    y_buf,
    z_buf,
    z_split,
    z_own,
    z_margin,
    z_sum,
    send_buf,
    recv_buf,
    g_buf,
    g_full,
    part_out,
    part_in,
    row_in,
    pick_out,
    pick_in,
    s_cols,
    s_neigh,
    s_lists,
    s_owner,
    load_sem,
    op_sem,
    table_sem,
    panel_send,
    panel_recv,
    z_send,
    z_recv,
    margin_send,
    margin_recv,
    part_send,
    part_recv,
    row_send,
    row_recv,
    pick_send,
    pick_recv,
):
    subs, grps, wide, tall, blocks, width, nt = sizes
    lanes = 128
    own_blocks = blocks * grps
    total_cols = own_blocks + 6 * SEND_COUNT
    n_tiles = blocks * nt
    rows = width // grps
    pairs = blocks // 2
    own_pairs = own_blocks // 2
    margin_pairs = SEND_COUNT // 2

    i = lax.axis_index("sub")
    g = lax.axis_index("grp")
    row, col = i // wide, i % wide
    parity = lax.rem(g, 2)

    def grp_peer(step):
        return lax.rem(g + step + grps, grps)

    op_copies = [
        pltpu.make_async_copy(tiles.at[0, b], op.at[b], op_sem.at[b]) for b in range(blocks)
    ]
    table_copies = [
        pltpu.make_async_copy(cols, s_cols, table_sem.at[0]),
        pltpu.make_async_copy(neigh, s_neigh, table_sem.at[1]),
        pltpu.make_async_copy(lists, s_lists, table_sem.at[2]),
        pltpu.make_async_copy(owner, s_owner, table_sem.at[3]),
    ]
    own_copy = pltpu.make_async_copy(defl.at[0], mine, load_sem)
    own_copy.start()
    for copy in op_copies + table_copies:
        copy.start()

    low_lanes = lax.broadcasted_iota(jnp.int32, (width, lanes), 1) < lanes // 2

    def halves(first, second):
        turned_first = pltpu.roll(first, lanes // 2, 1)
        turned_second = pltpu.roll(second, lanes // 2, 1)
        low = jnp.where(low_lanes, first, turned_second)
        high = jnp.where(low_lanes, turned_first, second)
        return low.astype(jnp.bfloat16), high.astype(jnp.bfloat16)

    barrier = pltpu.get_barrier_semaphore()
    for step in range(1, grps):
        pl.semaphore_signal(barrier, inc=1, device_id=(i, grp_peer(step)), device_id_type=MESH)
    for step in range(1, wide):
        other = row * wide + lax.rem(col + step, wide)
        pl.semaphore_signal(barrier, inc=1, device_id=(other, g), device_id_type=MESH)
    for step in range(1, tall):
        other = lax.rem(row + step, tall) * wide + col
        pl.semaphore_signal(barrier, inc=1, device_id=(other, g), device_id_type=MESH)
    expected = grps + wide + tall - 3
    for off in OFFSETS:
        there = i + off
        valid = (there >= 0) & (there < subs)

        @pl.when(valid)
        def _():
            pl.semaphore_signal(barrier, inc=1, device_id=(there, g), device_id_type=MESH)

        expected = expected + valid.astype(jnp.int32)
    own_copy.wait()
    for p in range(pairs):
        first, second = mine[2 * p].astype(jnp.float32), mine[2 * p + 1].astype(jnp.float32)
        split[0, p], split[1, p] = halves(first, second)
    pl.semaphore_wait(barrier, expected)

    def panel_copy(step):
        return pltpu.make_async_remote_copy(
            src_ref=split.at[lax.rem(g + step, 2)],
            dst_ref=half_panel.at[pl.ds(g * pairs, pairs)],
            send_sem=panel_send.at[step],
            recv_sem=panel_recv.at[step],
            device_id=(i, grp_peer(step)),
            device_id_type=MESH,
        )

    def panel_arrival(step):
        place = half_panel.at[pl.ds(grp_peer(-step) * pairs, pairs)]
        return pltpu.make_async_remote_copy(
            src_ref=place,
            dst_ref=place,
            send_sem=panel_send.at[step],
            recv_sem=panel_recv.at[step],
            device_id=(i, grp_peer(step)),
            device_id_type=MESH,
        )

    near_first = sorted(range(1, grps), key=lambda s: min(s, grps - s))
    for step in reversed(near_first):
        panel_copy(step).start()

    def products(b):
        op_copies[b].wait()
        left = mine[b]
        for t in range(nt):
            y_buf[pl.ds((b * nt + t) * width, width), :] = jnp.dot(
                left, op[b, t], preferred_element_type=jnp.float32
            )

    def by_column(first, last, picker):
        for a in range(first, last):
            by_tile = y_buf[pl.ds(a, n_tiles, stride=width), :].astype(jnp.bfloat16)
            z_buf[pl.ds(a, total_cols, stride=width), :] = jnp.dot(
                picker, by_tile, preferred_element_type=jnp.float32
            )

    for b in range(blocks):
        products(b)
    for copy in table_copies:
        copy.wait()
    lane_of = lax.broadcasted_iota(jnp.int32, (8, lanes), 1)
    named = jnp.full((8, lanes), -1, jnp.int32)
    for b in range(blocks):
        for t in range(nt):
            named = jnp.where(lane_of == b * nt + t, s_cols[b, 0, t], named)
    moved = named
    for r in range(6):
        low = own_blocks + r * SEND_COUNT
        within = (named >= low) & (named < low + SEND_COUNT)
        moved = moved + jnp.where(within, (s_neigh[0, r] - r) * SEND_COUNT, 0)
    named = jnp.broadcast_to(moved[0:1, :], (total_cols, lanes))
    hits = lax.broadcasted_iota(jnp.int32, (total_cols, lanes), 0) == named
    picker = jnp.where(hits, 1.0, 0.0).astype(jnp.bfloat16)[:, :n_tiles]
    by_column(0, width, picker)
    for p in range(total_cols // 2):
        first = z_buf[pl.ds(2 * p * width, width), :]
        second = z_buf[pl.ds((2 * p + 1) * width, width), :]
        z_split[0, p], z_split[1, p] = halves(first, second)

    def z_copy(which):
        first, count = (0, own_pairs) if which == 0 else (own_pairs, 6 * margin_pairs)
        return pltpu.make_async_remote_copy(
            src_ref=z_split.at[1 - parity, pl.ds(first, count)],
            dst_ref=(z_own, z_margin)[which],
            send_sem=z_send.at[which],
            recv_sem=z_recv.at[which],
            device_id=(i, grp_peer(2 * which - 1)),
            device_id_type=MESH,
        )

    z_copy(0).start()
    z_copy(1).start()

    def spread_blocks(origin):
        for p in range(pairs):
            packed = half_panel[origin * pairs + p].astype(jnp.float32)
            turned = pltpu.roll(packed, lanes // 2, 1)
            spread[origin * blocks + 2 * p] = jnp.where(low_lanes, packed, turned)
            spread[origin * blocks + 2 * p + 1] = jnp.where(low_lanes, turned, packed)

    for p in range(pairs):
        half_panel[g * pairs + p] = split[parity, p]
    spread_blocks(g)
    for step in near_first:
        panel_arrival(step).wait_recv()
        spread_blocks(grp_peer(-step))

    def margin(o):
        there = i - OFFSETS[o]
        return pltpu.make_async_remote_copy(
            src_ref=send_buf.at[o],
            dst_ref=recv_buf.at[o],
            send_sem=margin_send.at[o],
            recv_sem=margin_recv.at[o],
            device_id=(there, g),
            device_id_type=MESH,
        )

    def inside(there):
        return (there >= 0) & (there < subs)

    for o in ORDER:
        for p in range(margin_pairs):
            first, second = spread[s_lists[o, 0, 2 * p]], spread[s_lists[o, 0, 2 * p + 1]]
            send_buf[o, p] = jnp.where(low_lanes, first, second).astype(jnp.bfloat16)

        @pl.when(inside(i - OFFSETS[o]))
        def _():
            margin(o).start()

    def contract(left, right):
        return lax.dot_general(
            jnp.concatenate(left, axis=1),
            jnp.concatenate(right, axis=1),
            (((1,), (1,)), ((), ())),
            preferred_element_type=jnp.float32,
        )

    g_buf[...] = jnp.zeros_like(g_buf)
    part_out[...] = jnp.zeros_like(part_out)
    g_full[...] = jnp.zeros_like(g_full)
    chosen = []
    for target in range(tall):
        place = jnp.int32(0)
        for c in range(1, wide):
            place = jnp.where(s_owner[row * wide + c] == target * wide + col, c, place)
        chosen.append(place)
    origin_row = jnp.int32(0)
    for s in range(subs):
        origin_row = jnp.where(s_owner[s] == i, s // wide, origin_row)

    def both(theirs, p, q):
        total = z_split[parity, p].astype(jnp.float32) + theirs[q].astype(jnp.float32)
        return total.astype(jnp.bfloat16)

    z_copy(0).wait_recv()
    own = jnp.zeros((width, width), jnp.float32)
    for origin in range(grps):
        places = range(origin * pairs, (origin + 1) * pairs)
        own = own + contract([both(z_own, p, p) for p in places], [half_panel[p] for p in places])
    g_full[:, pl.ds(0, width)] = own
    z_copy(1).wait_recv()
    for p in range(6 * margin_pairs):
        z_sum[p] = both(z_margin, own_pairs + p, p)

    for o in ORDER:

        @pl.when(inside(i + OFFSETS[o]))
        def _():
            margin(o).wait_recv()
            places = range(margin_pairs)
            g_buf[o] = contract(
                [z_sum[o * margin_pairs + p] for p in places], [recv_buf[o, p] for p in places]
            )

    for r in range(6):
        slot = s_neigh[0, r]
        value = g_buf[jnp.maximum(slot, 0)]
        g_full[:, pl.ds((r + 1) * width, width)] = jnp.where(
            jnp.full((width, width), slot) >= 0, value, 0.0
        )

    spans = -(-7 * width // lanes)
    for other in range(grps):
        for span in range(spans):
            part_out[other, pl.ds(span * rows, rows), :] = g_full[
                pl.ds(other * rows, rows), pl.ds(span * lanes, lanes)
            ]

    def part(step):
        return pltpu.make_async_remote_copy(
            src_ref=part_out.at[grp_peer(step)],
            dst_ref=part_in.at[step],
            send_sem=part_send.at[step],
            recv_sem=part_recv.at[step],
            device_id=(i, grp_peer(step)),
            device_id_type=MESH,
        )

    for step in reversed(near_first):
        part(step).start()
    summed = part_out[g]
    for step in near_first:
        part(step).wait_recv()
        summed = summed + part_in[step]

    row_in[0] = summed

    def across(step):
        return pltpu.make_async_remote_copy(
            src_ref=row_in.at[0],
            dst_ref=row_in.at[step],
            send_sem=row_send.at[step],
            recv_sem=row_recv.at[step],
            device_id=(row * wide + lax.rem(col + step, wide), g),
            device_id_type=MESH,
        )

    for step in range(1, wide):
        across(step).start()
    for step in range(1, wide):
        across(step).wait_recv()
    for target in range(tall):
        pick_out[target] = row_in[lax.rem(col - chosen[target] + wide, wide)]

    def along(step):
        return pltpu.make_async_remote_copy(
            src_ref=pick_out.at[lax.rem(row + step, tall)],
            dst_ref=pick_in.at[step],
            send_sem=pick_send.at[step],
            recv_sem=pick_recv.at[step],
            device_id=(lax.rem(row + step, tall) * wide + col, g),
            device_id_type=MESH,
        )

    for step in range(1, tall):
        along(step).start()
    pick_in[0] = pick_out[row]
    for step in range(1, tall):
        along(step).wait_recv()
    final = pick_in[lax.rem(row - origin_row + tall, tall)]
    for span in range(spans):
        count = min(lanes, 7 * width - span * lanes)
        out[:, 0, pl.ds(span * lanes, count)] = final[span * rows : (span + 1) * rows, :count]

    for step in range(1, grps):
        panel_copy(step).wait_send()
    z_copy(0).wait_send()
    z_copy(1).wait_send()
    for o in ORDER:

        @pl.when(inside(i - OFFSETS[o]))
        def _():
            margin(o).wait_send()

    for step in range(1, grps):
        part(step).wait_send()
    for step in range(1, wide):
        across(step).wait_send()
    for step in range(1, tall):
        along(step).wait_send()


def shards(deflation, operator_tiles, tile_columns, neighbours, send_blocks, row_owner):
    subs, grps = lax.axis_size("sub"), lax.axis_size("grp")
    wide = 1 << (subs.bit_length() // 2)
    tall = subs // wide
    _, blocks, width, lanes = deflation.shape
    nt = operator_tiles.shape[2]
    own_blocks = blocks * grps
    total_cols = own_blocks + 6 * SEND_COUNT
    spans = -(-7 * width // lanes)
    rows = width // grps
    packed = -(-spans * rows // 8) * 8
    bf16, f32, i32 = jnp.bfloat16, jnp.float32, jnp.int32
    dma = pltpu.SemaphoreType.DMA
    sizes = (subs, grps, wide, tall, blocks, width, nt)
    result = pl.pallas_call(
        functools.partial(kernel, sizes),
        out_shape=jax.ShapeDtypeStruct((rows, 1, 7 * width), f32),
        in_specs=[pl.BlockSpec(memory_space=pltpu.HBM)] * 6,
        out_specs=pl.BlockSpec(memory_space=pltpu.VMEM),
        scratch_shapes=[
            pltpu.VMEM((blocks, width, lanes), bf16),
            pltpu.VMEM((2, blocks // 2, width, lanes), bf16),
            pltpu.VMEM((own_blocks // 2, width, lanes), bf16),
            pltpu.VMEM((own_blocks, width, lanes), f32),
            pltpu.VMEM((blocks, nt, lanes, lanes), bf16),
            pltpu.VMEM((blocks * nt * width, lanes), f32),
            pltpu.VMEM((total_cols * width, lanes), f32),
            pltpu.VMEM((2, total_cols // 2, width, lanes), bf16),
            pltpu.VMEM((own_blocks // 2, width, lanes), bf16),
            pltpu.VMEM((3 * SEND_COUNT, width, lanes), bf16),
            pltpu.VMEM((3 * SEND_COUNT, width, lanes), bf16),
            pltpu.VMEM((6, SEND_COUNT // 2, width, lanes), bf16),
            pltpu.VMEM((6, SEND_COUNT // 2, width, lanes), bf16),
            pltpu.VMEM((6, width, width), f32),
            pltpu.VMEM((width, spans * lanes), f32),
            pltpu.VMEM((grps, packed, lanes), f32),
            pltpu.VMEM((grps, packed, lanes), f32),
            pltpu.VMEM((wide, packed, lanes), f32),
            pltpu.VMEM((tall, packed, lanes), f32),
            pltpu.VMEM((tall, packed, lanes), f32),
            pltpu.SMEM((blocks, 1, nt), i32),
            pltpu.SMEM((1, 6), i32),
            pltpu.SMEM((6, 1, SEND_COUNT), i32),
            pltpu.SMEM((subs,), i32),
            dma,
            dma((blocks,)),
            dma((4,)),
            dma((grps,)),
            dma((grps,)),
            dma((2,)),
            dma((2,)),
            dma((6,)),
            dma((6,)),
            dma((grps,)),
            dma((grps,)),
            dma((wide,)),
            dma((wide,)),
            dma((tall,)),
            dma((tall,)),
        ],
        compiler_params=pltpu.CompilerParams(
            collective_id=0, has_side_effects=True, vmem_limit_bytes=60 * 2**20
        ),
    )(
        deflation,
        operator_tiles,
        tile_columns.reshape(blocks, 1, nt),
        neighbours,
        send_blocks.reshape(6, 1, SEND_COUNT),
        row_owner,
    )
    return result.reshape(1, rows, 7 * width)


def solution(mesh):
    placed = (
        P("sub", "grp", None, None),
        P("sub", "grp", None, None, None),
        P("sub", "grp", None),
        P("sub", None),
        P("sub", None, None),
        P(),
    )
    return jax.shard_map(
        shards, mesh=mesh, in_specs=placed, out_specs=P("sub", "grp", None), check_vma=False
    )
```

```python
import functools

import jax
import jax.numpy as jnp
from jax import lax
from jax.experimental import pallas as pl
from jax.experimental.pallas import tpu as pltpu
from jax.sharding import PartitionSpec as P

OFFSETS = (1, 2, 3, -1, -2, -3)
ORDER = (2, 5, 1, 4, 0, 3)
SEND_COUNT = 8
MESH = pl.DeviceIdType.MESH


def reaches_of(subs):
    return [1 << level for level in range(1, max(1, subs.bit_length() - 2))]


def kernel(
    sizes,
    defl,
    tiles,
    cols,
    neigh,
    lists,
    owner,
    out,
    mine,
    split,
    half_panel,
    spread,
    op,
    y_buf,
    z_buf,
    z_split,
    z_own,
    z_margin,
    z_sum,
    send_buf,
    recv_buf,
    g_buf,
    g_full,
    part_out,
    part_in,
    row_in,
    pick_out,
    pick_in,
    s_cols,
    s_neigh,
    s_lists,
    s_owner,
    load_sem,
    op_sem,
    table_sem,
    panel_send,
    panel_recv,
    z_send,
    z_recv,
    margin_send,
    margin_recv,
    part_send,
    part_recv,
    row_send,
    row_recv,
    pick_send,
    pick_recv,
    greet_sem,
):
    subs, grps, wide, tall, blocks, width, nt = sizes
    lanes = 128
    own_blocks = blocks * grps
    total_cols = own_blocks + 6 * SEND_COUNT
    n_tiles = blocks * nt
    reaches = reaches_of(subs)
    rows = width // grps
    pairs = blocks // 2
    own_pairs = own_blocks // 2
    margin_pairs = SEND_COUNT // 2

    i = lax.axis_index("sub")
    g = lax.axis_index("grp")
    row, col = i // wide, i % wide
    parity = lax.rem(g, 2)

    def grp_peer(step):
        return lax.rem(g + step + grps, grps)

    def sub_peer(step):
        return lax.rem(i + step + subs, subs)

    def greet(level):
        if level < len(reaches):
            for step in (reaches[level], -reaches[level]):
                pl.semaphore_signal(
                    greet_sem.at[level], inc=1, device_id=(sub_peer(step), g), device_id_type=MESH
                )

    def greeted(level):
        if level < len(reaches):
            pl.semaphore_wait(greet_sem.at[level], 2)

    op_copies = [
        pltpu.make_async_copy(tiles.at[0, b], op.at[b], op_sem.at[b]) for b in range(blocks)
    ]
    table_copies = [
        pltpu.make_async_copy(cols, s_cols, table_sem.at[0]),
        pltpu.make_async_copy(neigh, s_neigh, table_sem.at[1]),
        pltpu.make_async_copy(lists, s_lists, table_sem.at[2]),
        pltpu.make_async_copy(owner, s_owner, table_sem.at[3]),
    ]
    own_copy = pltpu.make_async_copy(defl.at[0], mine, load_sem)
    own_copy.start()

    low_lanes = lax.broadcasted_iota(jnp.int32, (width, lanes), 1) < lanes // 2

    def halves(first, second):
        turned_first = pltpu.roll(first, lanes // 2, 1)
        turned_second = pltpu.roll(second, lanes // 2, 1)
        low = jnp.where(low_lanes, first, turned_second)
        high = jnp.where(low_lanes, turned_first, second)
        return low.astype(jnp.bfloat16), high.astype(jnp.bfloat16)

    barrier = pltpu.get_barrier_semaphore()
    for step in range(1, grps):
        pl.semaphore_signal(barrier, inc=1, device_id=(i, grp_peer(step)), device_id_type=MESH)
    for step in (1, -1, 2, -2):
        pl.semaphore_signal(barrier, inc=1, device_id=(sub_peer(step), g), device_id_type=MESH)
    own_copy.wait()
    for p in range(pairs):
        first, second = mine[2 * p].astype(jnp.float32), mine[2 * p + 1].astype(jnp.float32)
        split[0, p], split[1, p] = halves(first, second)
    pl.semaphore_wait(barrier, grps + 3)

    def panel_copy(step):
        return pltpu.make_async_remote_copy(
            src_ref=split.at[lax.rem(g + step, 2)],
            dst_ref=half_panel.at[pl.ds(g * pairs, pairs)],
            send_sem=panel_send.at[step],
            recv_sem=panel_recv.at[step],
            device_id=(i, grp_peer(step)),
            device_id_type=MESH,
        )

    def panel_arrival(step):
        place = half_panel.at[pl.ds(grp_peer(-step) * pairs, pairs)]
        return pltpu.make_async_remote_copy(
            src_ref=place,
            dst_ref=place,
            send_sem=panel_send.at[step],
            recv_sem=panel_recv.at[step],
            device_id=(i, grp_peer(step)),
            device_id_type=MESH,
        )

    near_first = sorted(range(1, grps), key=lambda s: min(s, grps - s))
    for step in reversed(near_first):
        panel_copy(step).start()
    greet(0)
    for copy in op_copies + table_copies:
        copy.start()

    def products(b):
        op_copies[b].wait()
        left = mine[b]
        for t in range(nt):
            y_buf[pl.ds((b * nt + t) * width, width), :] = jnp.dot(
                left, op[b, t], preferred_element_type=jnp.float32
            )

    def by_column(first, last, picker):
        for a in range(first, last):
            by_tile = y_buf[pl.ds(a, n_tiles, stride=width), :].astype(jnp.bfloat16)
            z_buf[pl.ds(a, total_cols, stride=width), :] = jnp.dot(
                picker, by_tile, preferred_element_type=jnp.float32
            )

    for b in range(blocks):
        products(b)
    greeted(0)
    greet(1)
    for copy in table_copies:
        copy.wait()
    lane_of = lax.broadcasted_iota(jnp.int32, (8, lanes), 1)
    named = jnp.full((8, lanes), -1, jnp.int32)
    for b in range(blocks):
        for t in range(nt):
            named = jnp.where(lane_of == b * nt + t, s_cols[b, 0, t], named)
    moved = named
    for r in range(6):
        low = own_blocks + r * SEND_COUNT
        within = (named >= low) & (named < low + SEND_COUNT)
        moved = moved + jnp.where(within, (s_neigh[0, r] - r) * SEND_COUNT, 0)
    named = jnp.broadcast_to(moved[0:1, :], (total_cols, lanes))
    hits = lax.broadcasted_iota(jnp.int32, (total_cols, lanes), 0) == named
    picker = jnp.where(hits, 1.0, 0.0).astype(jnp.bfloat16)[:, :n_tiles]
    by_column(0, width, picker)
    for p in range(total_cols // 2):
        first = z_buf[pl.ds(2 * p * width, width), :]
        second = z_buf[pl.ds((2 * p + 1) * width, width), :]
        z_split[0, p], z_split[1, p] = halves(first, second)

    def z_copy(which):
        first, count = (0, own_pairs) if which == 0 else (own_pairs, 6 * margin_pairs)
        return pltpu.make_async_remote_copy(
            src_ref=z_split.at[1 - parity, pl.ds(first, count)],
            dst_ref=(z_own, z_margin)[which],
            send_sem=z_send.at[which],
            recv_sem=z_recv.at[which],
            device_id=(i, grp_peer(2 * which - 1)),
            device_id_type=MESH,
        )

    z_copy(0).start()
    z_copy(1).start()
    greeted(1)
    greet(2)

    def spread_blocks(origin):
        for p in range(pairs):
            packed = half_panel[origin * pairs + p].astype(jnp.float32)
            turned = pltpu.roll(packed, lanes // 2, 1)
            spread[origin * blocks + 2 * p] = jnp.where(low_lanes, packed, turned)
            spread[origin * blocks + 2 * p + 1] = jnp.where(low_lanes, turned, packed)

    for p in range(pairs):
        half_panel[g * pairs + p] = split[parity, p]
    spread_blocks(g)
    for step in near_first:
        panel_arrival(step).wait_recv()
        spread_blocks(grp_peer(-step))

    def margin(o):
        there = i - OFFSETS[o]
        return pltpu.make_async_remote_copy(
            src_ref=send_buf.at[o],
            dst_ref=recv_buf.at[o],
            send_sem=margin_send.at[o],
            recv_sem=margin_recv.at[o],
            device_id=(there, g),
            device_id_type=MESH,
        )

    def inside(there):
        return (there >= 0) & (there < subs)

    for o in ORDER:
        for p in range(margin_pairs):
            first, second = spread[s_lists[o, 0, 2 * p]], spread[s_lists[o, 0, 2 * p + 1]]
            send_buf[o, p] = jnp.where(low_lanes, first, second).astype(jnp.bfloat16)

        @pl.when(inside(i - OFFSETS[o]))
        def _():
            margin(o).start()

    def contract(left, right):
        return lax.dot_general(
            jnp.concatenate(left, axis=1),
            jnp.concatenate(right, axis=1),
            (((1,), (1,)), ((), ())),
            preferred_element_type=jnp.float32,
        )

    greeted(2)
    greet(3)
    for o in range(6):

        @pl.when(jnp.logical_not(inside(i + OFFSETS[o])))
        def _():
            recv_buf[o] = jnp.zeros_like(recv_buf[o])

    part_out[...] = jnp.zeros_like(part_out)
    g_full[...] = jnp.zeros_like(g_full)
    chosen = []
    for target in range(tall):
        place = jnp.int32(0)
        for c in range(1, wide):
            place = jnp.where(s_owner[row * wide + c] == target * wide + col, c, place)
        chosen.append(place)
    origin_row = jnp.int32(0)
    for s in range(subs):
        origin_row = jnp.where(s_owner[s] == i, s // wide, origin_row)

    def both(theirs, p, q):
        total = z_split[parity, p].astype(jnp.float32) + theirs[q].astype(jnp.float32)
        return total.astype(jnp.bfloat16)

    z_copy(0).wait_recv()
    own = jnp.zeros((width, width), jnp.float32)
    for origin in range(grps):
        places = range(origin * pairs, (origin + 1) * pairs)
        own = own + contract([both(z_own, p, p) for p in places], [half_panel[p] for p in places])
    g_full[:, pl.ds(0, width)] = own
    z_copy(1).wait_recv()
    for p in range(6 * margin_pairs):
        z_sum[p] = both(z_margin, own_pairs + p, p)

    for o in ORDER:

        @pl.when(inside(i + OFFSETS[o]))
        def _():
            margin(o).wait_recv()

    places = range(margin_pairs)
    for o in range(6):
        g_buf[o] = contract(
            [z_sum[o * margin_pairs + p] for p in places], [recv_buf[o, p] for p in places]
        )

    for r in range(6):
        slot = s_neigh[0, r]
        value = g_buf[jnp.maximum(slot, 0)]
        g_full[:, pl.ds((r + 1) * width, width)] = jnp.where(
            jnp.full((width, width), slot) >= 0, value, 0.0
        )

    spans = -(-7 * width // lanes)
    for other in range(grps):
        for span in range(spans):
            part_out[other, pl.ds(span * rows, rows), :] = g_full[
                pl.ds(other * rows, rows), pl.ds(span * lanes, lanes)
            ]

    greeted(3)

    def part(step):
        return pltpu.make_async_remote_copy(
            src_ref=part_out.at[grp_peer(step)],
            dst_ref=part_in.at[step],
            send_sem=part_send.at[step],
            recv_sem=part_recv.at[step],
            device_id=(i, grp_peer(step)),
            device_id_type=MESH,
        )

    for step in reversed(near_first):
        part(step).start()
    for step in range(1, grps):
        panel_copy(step).wait_send()
    z_copy(0).wait_send()
    z_copy(1).wait_send()
    for o in ORDER:

        @pl.when(inside(i - OFFSETS[o]))
        def _():
            margin(o).wait_send()

    summed = part_out[g]
    for step in near_first:
        part(step).wait_recv()
        summed = summed + part_in[step]

    row_in[0] = summed

    def across(step):
        return pltpu.make_async_remote_copy(
            src_ref=row_in.at[0],
            dst_ref=row_in.at[step],
            send_sem=row_send.at[step],
            recv_sem=row_recv.at[step],
            device_id=(row * wide + lax.rem(col + step, wide), g),
            device_id_type=MESH,
        )

    for step in range(1, wide):
        across(step).start()
    for step in range(1, grps):
        part(step).wait_send()
    for step in range(1, wide):
        across(step).wait_recv()
    for target in range(tall):
        pick_out[target] = row_in[lax.rem(col - chosen[target] + wide, wide)]

    def along(step):
        return pltpu.make_async_remote_copy(
            src_ref=pick_out.at[lax.rem(row + step, tall)],
            dst_ref=pick_in.at[step],
            send_sem=pick_send.at[step],
            recv_sem=pick_recv.at[step],
            device_id=(lax.rem(row + step, tall) * wide + col, g),
            device_id_type=MESH,
        )

    for step in range(1, tall):
        along(step).start()
    pick_in[0] = pick_out[row]
    for step in range(1, wide):
        across(step).wait_send()
    for step in range(1, tall):
        along(step).wait_recv()
    final = pick_in[lax.rem(row - origin_row + tall, tall)]
    for span in range(spans):
        count = min(lanes, 7 * width - span * lanes)
        out[:, 0, pl.ds(span * lanes, count)] = final[span * rows : (span + 1) * rows, :count]

    for step in range(1, tall):
        along(step).wait_send()


def shards(deflation, operator_tiles, tile_columns, neighbours, send_blocks, row_owner):
    subs, grps = lax.axis_size("sub"), lax.axis_size("grp")
    wide = 1 << (subs.bit_length() // 2)
    tall = subs // wide
    _, blocks, width, lanes = deflation.shape
    nt = operator_tiles.shape[2]
    own_blocks = blocks * grps
    total_cols = own_blocks + 6 * SEND_COUNT
    spans = -(-7 * width // lanes)
    rows = width // grps
    packed = -(-spans * rows // 8) * 8
    bf16, f32, i32 = jnp.bfloat16, jnp.float32, jnp.int32
    dma = pltpu.SemaphoreType.DMA
    sizes = (subs, grps, wide, tall, blocks, width, nt)
    result = pl.pallas_call(
        functools.partial(kernel, sizes),
        out_shape=jax.ShapeDtypeStruct((rows, 1, 7 * width), f32),
        in_specs=[pl.BlockSpec(memory_space=pltpu.HBM)] * 6,
        out_specs=pl.BlockSpec(memory_space=pltpu.VMEM),
        scratch_shapes=[
            pltpu.VMEM((blocks, width, lanes), bf16),
            pltpu.VMEM((2, blocks // 2, width, lanes), bf16),
            pltpu.VMEM((own_blocks // 2, width, lanes), bf16),
            pltpu.VMEM((own_blocks, width, lanes), f32),
            pltpu.VMEM((blocks, nt, lanes, lanes), bf16),
            pltpu.VMEM((blocks * nt * width, lanes), f32),
            pltpu.VMEM((total_cols * width, lanes), f32),
            pltpu.VMEM((2, total_cols // 2, width, lanes), bf16),
            pltpu.VMEM((own_blocks // 2, width, lanes), bf16),
            pltpu.VMEM((3 * SEND_COUNT, width, lanes), bf16),
            pltpu.VMEM((3 * SEND_COUNT, width, lanes), bf16),
            pltpu.VMEM((6, SEND_COUNT // 2, width, lanes), bf16),
            pltpu.VMEM((6, SEND_COUNT // 2, width, lanes), bf16),
            pltpu.VMEM((6, width, width), f32),
            pltpu.VMEM((width, spans * lanes), f32),
            pltpu.VMEM((grps, packed, lanes), f32),
            pltpu.VMEM((grps, packed, lanes), f32),
            pltpu.VMEM((wide, packed, lanes), f32),
            pltpu.VMEM((tall, packed, lanes), f32),
            pltpu.VMEM((tall, packed, lanes), f32),
            pltpu.SMEM((blocks, 1, nt), i32),
            pltpu.SMEM((1, 6), i32),
            pltpu.SMEM((6, 1, SEND_COUNT), i32),
            pltpu.SMEM((subs,), i32),
            dma,
            dma((blocks,)),
            dma((4,)),
            dma((grps,)),
            dma((grps,)),
            dma((2,)),
            dma((2,)),
            dma((6,)),
            dma((6,)),
            dma((grps,)),
            dma((grps,)),
            dma((wide,)),
            dma((wide,)),
            dma((tall,)),
            dma((tall,)),
            pltpu.SemaphoreType.REGULAR((max(1, len(reaches_of(subs))),)),
        ],
        compiler_params=pltpu.CompilerParams(
            collective_id=0, has_side_effects=True, vmem_limit_bytes=60 * 2**20
        ),
    )(
        deflation,
        operator_tiles,
        tile_columns.reshape(blocks, 1, nt),
        neighbours,
        send_blocks.reshape(6, 1, SEND_COUNT),
        row_owner,
    )
    return result.reshape(1, rows, 7 * width)


def solution(mesh):
    placed = (
        P("sub", "grp", None, None),
        P("sub", "grp", None, None, None),
        P("sub", "grp", None),
        P("sub", None),
        P("sub", None, None),
        P(),
    )
    return jax.shard_map(
        shards, mesh=mesh, in_specs=placed, out_specs=P("sub", "grp", None), check_vma=False
    )
```

```python
import functools

import jax
import jax.numpy as jnp
from jax import lax
from jax.experimental import pallas as pl
from jax.experimental.pallas import tpu as pltpu
from jax.sharding import PartitionSpec as P

OFFSETS = (1, 2, 3, -1, -2, -3)
ORDER = (2, 5, 1, 4, 0, 3)
SEND_COUNT = 8
MESH = pl.DeviceIdType.MESH


def reaches_of(subs):
    return [1 << level for level in range(1, max(1, subs.bit_length() - 2))]


def kernel(
    sizes,
    defl,
    tiles,
    cols,
    neigh,
    lists,
    owner,
    out,
    mine,
    split,
    half_panel,
    spread,
    op,
    y_buf,
    z_buf,
    z_split,
    z_own,
    z_margin,
    z_sum,
    send_buf,
    recv_buf,
    g_buf,
    g_full,
    part_out,
    part_in,
    row_in,
    pick_out,
    pick_in,
    s_cols,
    s_neigh,
    s_lists,
    s_owner,
    load_sem,
    op_sem,
    table_sem,
    panel_send,
    panel_recv,
    z_send,
    z_recv,
    margin_send,
    margin_recv,
    part_send,
    part_recv,
    row_send,
    row_recv,
    pick_send,
    pick_recv,
    greet_sem,
):
    subs, grps, wide, tall, blocks, width, nt = sizes
    lanes = 128
    own_blocks = blocks * grps
    total_cols = own_blocks + 6 * SEND_COUNT
    n_tiles = blocks * nt
    reaches = reaches_of(subs)
    rows = width // grps
    pairs = blocks // 2
    own_pairs = own_blocks // 2
    margin_pairs = SEND_COUNT // 2

    i = lax.axis_index("sub")
    g = lax.axis_index("grp")
    row, col = i // wide, i % wide
    parity = lax.rem(g, 2)

    def grp_peer(step):
        return lax.rem(g + step + grps, grps)

    def sub_peer(step):
        return lax.rem(i + step + subs, subs)

    def greet(level):
        if level < len(reaches):
            for step in (reaches[level], -reaches[level]):
                pl.semaphore_signal(
                    greet_sem.at[level], inc=1, device_id=(sub_peer(step), g), device_id_type=MESH
                )

    def greeted(level):
        if level < len(reaches):
            pl.semaphore_wait(greet_sem.at[level], 2)

    op_copies = [
        pltpu.make_async_copy(tiles.at[0, b], op.at[b], op_sem.at[b]) for b in range(blocks)
    ]
    table_copies = [
        pltpu.make_async_copy(cols, s_cols, table_sem.at[0]),
        pltpu.make_async_copy(neigh, s_neigh, table_sem.at[1]),
        pltpu.make_async_copy(lists, s_lists, table_sem.at[2]),
        pltpu.make_async_copy(owner, s_owner, table_sem.at[3]),
    ]
    own_copy = pltpu.make_async_copy(defl.at[0], mine, load_sem)
    own_copy.start()

    low_lanes = lax.broadcasted_iota(jnp.int32, (width, lanes), 1) < lanes // 2

    def halves(first, second):
        turned_first = pltpu.roll(first, lanes // 2, 1)
        turned_second = pltpu.roll(second, lanes // 2, 1)
        low = jnp.where(low_lanes, first, turned_second)
        high = jnp.where(low_lanes, turned_first, second)
        return low.astype(jnp.bfloat16), high.astype(jnp.bfloat16)

    barrier = pltpu.get_barrier_semaphore()
    for step in range(1, grps):
        pl.semaphore_signal(barrier, inc=1, device_id=(i, grp_peer(step)), device_id_type=MESH)
    for step in (1, -1, 2, -2):
        pl.semaphore_signal(barrier, inc=1, device_id=(sub_peer(step), g), device_id_type=MESH)
    own_copy.wait()
    for p in range(pairs):
        first, second = mine[2 * p].astype(jnp.float32), mine[2 * p + 1].astype(jnp.float32)
        split[0, p], split[1, p] = halves(first, second)
    pl.semaphore_wait(barrier, grps + 3)

    def panel_copy(step):
        return pltpu.make_async_remote_copy(
            src_ref=split.at[lax.rem(g + step, 2)],
            dst_ref=half_panel.at[pl.ds(g * pairs, pairs)],
            send_sem=panel_send.at[step],
            recv_sem=panel_recv.at[step],
            device_id=(i, grp_peer(step)),
            device_id_type=MESH,
        )

    def panel_arrival(step):
        place = half_panel.at[pl.ds(grp_peer(-step) * pairs, pairs)]
        return pltpu.make_async_remote_copy(
            src_ref=place,
            dst_ref=place,
            send_sem=panel_send.at[step],
            recv_sem=panel_recv.at[step],
            device_id=(i, grp_peer(step)),
            device_id_type=MESH,
        )

    near_first = sorted(range(1, grps), key=lambda s: min(s, grps - s))
    for step in reversed(near_first):
        panel_copy(step).start()
    greet(0)
    for copy in op_copies + table_copies:
        copy.start()

    def products(b):
        op_copies[b].wait()
        left = mine[b]
        for t in range(nt):
            y_buf[pl.ds((b * nt + t) * width, width), :] = jnp.dot(
                left, op[b, t], preferred_element_type=jnp.float32
            )

    def by_column(first, last, picker):
        for a in range(first, last):
            by_tile = y_buf[pl.ds(a, n_tiles, stride=width), :].astype(jnp.bfloat16)
            z_buf[pl.ds(a, total_cols, stride=width), :] = jnp.dot(
                picker, by_tile, preferred_element_type=jnp.float32
            )

    for b in range(blocks):
        products(b)
    greeted(0)
    greet(1)
    for copy in table_copies:
        copy.wait()
    lane_of = lax.broadcasted_iota(jnp.int32, (8, lanes), 1)
    named = jnp.full((8, lanes), -1, jnp.int32)
    for b in range(blocks):
        for t in range(nt):
            named = jnp.where(lane_of == b * nt + t, s_cols[b, 0, t], named)
    moved = named
    for r in range(6):
        low = own_blocks + r * SEND_COUNT
        within = (named >= low) & (named < low + SEND_COUNT)
        moved = moved + jnp.where(within, (s_neigh[0, r] - r) * SEND_COUNT, 0)
    named = jnp.broadcast_to(moved[0:1, :], (total_cols, lanes))
    hits = lax.broadcasted_iota(jnp.int32, (total_cols, lanes), 0) == named
    picker = jnp.where(hits, 1.0, 0.0).astype(jnp.bfloat16)[:, :n_tiles]
    by_column(0, width, picker)
    for p in range(total_cols // 2):
        first = z_buf[pl.ds(2 * p * width, width), :]
        second = z_buf[pl.ds((2 * p + 1) * width, width), :]
        z_split[0, p], z_split[1, p] = halves(first, second)

    def z_copy(which):
        first, count = (0, own_pairs) if which == 0 else (own_pairs, 6 * margin_pairs)
        return pltpu.make_async_remote_copy(
            src_ref=z_split.at[1 - parity, pl.ds(first, count)],
            dst_ref=(z_own, z_margin)[which],
            send_sem=z_send.at[which],
            recv_sem=z_recv.at[which],
            device_id=(i, grp_peer(2 * which - 1)),
            device_id_type=MESH,
        )

    z_copy(0).start()
    z_copy(1).start()
    greeted(1)
    greet(2)

    def spread_blocks(origin):
        for p in range(pairs):
            packed = half_panel[origin * pairs + p].astype(jnp.float32)
            turned = pltpu.roll(packed, lanes // 2, 1)
            spread[origin * blocks + 2 * p] = jnp.where(low_lanes, packed, turned)
            spread[origin * blocks + 2 * p + 1] = jnp.where(low_lanes, turned, packed)

    for p in range(pairs):
        half_panel[g * pairs + p] = split[parity, p]
    spread_blocks(g)
    for step in near_first:
        panel_arrival(step).wait_recv()
        spread_blocks(grp_peer(-step))

    def margin(o):
        there = i - OFFSETS[o]
        return pltpu.make_async_remote_copy(
            src_ref=send_buf.at[o],
            dst_ref=recv_buf.at[o],
            send_sem=margin_send.at[o],
            recv_sem=margin_recv.at[o],
            device_id=(there, g),
            device_id_type=MESH,
        )

    def inside(there):
        return (there >= 0) & (there < subs)

    for o in ORDER:
        for p in range(margin_pairs):
            first, second = spread[s_lists[o, 0, 2 * p]], spread[s_lists[o, 0, 2 * p + 1]]
            send_buf[o, p] = jnp.where(low_lanes, first, second).astype(jnp.bfloat16)

        @pl.when(inside(i - OFFSETS[o]))
        def _():
            margin(o).start()

    def contract(left, right):
        return lax.dot_general(
            jnp.concatenate(left, axis=1),
            jnp.concatenate(right, axis=1),
            (((1,), (1,)), ((), ())),
            preferred_element_type=jnp.float32,
        )

    greeted(2)
    greet(3)
    for o in range(6):

        @pl.when(jnp.logical_not(inside(i + OFFSETS[o])))
        def _():
            recv_buf[o] = jnp.zeros_like(recv_buf[o])

    part_out[...] = jnp.zeros_like(part_out)
    g_full[...] = jnp.zeros_like(g_full)
    chosen = []
    for target in range(tall):
        place = jnp.int32(0)
        for c in range(1, wide):
            place = jnp.where(s_owner[row * wide + c] == target * wide + col, c, place)
        chosen.append(place)
    origin_row = jnp.int32(0)
    for s in range(subs):
        origin_row = jnp.where(s_owner[s] == i, s // wide, origin_row)

    def both(theirs, p, q):
        total = z_split[parity, p].astype(jnp.float32) + theirs[q].astype(jnp.float32)
        return total.astype(jnp.bfloat16)

    z_copy(0).wait_recv()
    own = jnp.zeros((width, width), jnp.float32)
    for origin in range(grps):
        places = range(origin * pairs, (origin + 1) * pairs)
        own = own + contract([both(z_own, p, p) for p in places], [half_panel[p] for p in places])
    g_full[:, pl.ds(0, width)] = own
    z_copy(1).wait_recv()
    for p in range(6 * margin_pairs):
        z_sum[p] = both(z_margin, own_pairs + p, p)

    for o in ORDER:

        @pl.when(inside(i + OFFSETS[o]))
        def _():
            margin(o).wait_recv()

    places = range(margin_pairs)
    for o in range(6):
        g_buf[o] = contract(
            [z_sum[o * margin_pairs + p] for p in places], [recv_buf[o, p] for p in places]
        )

    for r in range(6):
        slot = s_neigh[0, r]
        value = g_buf[jnp.maximum(slot, 0)]
        g_full[:, pl.ds((r + 1) * width, width)] = jnp.where(
            jnp.full((width, width), slot) >= 0, value, 0.0
        )

    spans = -(-7 * width // lanes)
    for other in range(grps):
        for span in range(spans):
            part_out[other, pl.ds(span * rows, rows), :] = g_full[
                pl.ds(other * rows, rows), pl.ds(span * lanes, lanes)
            ]

    greeted(3)

    def part(step):
        return pltpu.make_async_remote_copy(
            src_ref=part_out.at[grp_peer(step)],
            dst_ref=part_in.at[step],
            send_sem=part_send.at[step],
            recv_sem=part_recv.at[step],
            device_id=(i, grp_peer(step)),
            device_id_type=MESH,
        )

    for step in reversed(near_first):
        part(step).start()
    for step in range(1, grps):
        panel_copy(step).wait_send()
    z_copy(0).wait_send()
    z_copy(1).wait_send()
    for o in ORDER:

        @pl.when(inside(i - OFFSETS[o]))
        def _():
            margin(o).wait_send()

    summed = part_out[g]
    for step in near_first:
        part(step).wait_recv()
        summed = summed + part_in[step]

    row_in[0] = summed

    def across(step):
        return pltpu.make_async_remote_copy(
            src_ref=row_in.at[0],
            dst_ref=row_in.at[step],
            send_sem=row_send.at[step],
            recv_sem=row_recv.at[step],
            device_id=(row * wide + lax.rem(col + step, wide), g),
            device_id_type=MESH,
        )

    for step in range(1, wide):
        across(step).start()
    for step in range(1, grps):
        part(step).wait_send()
    for step in range(1, wide):
        across(step).wait_recv()
    for target in range(tall):
        pick_out[target] = row_in[lax.rem(col - chosen[target] + wide, wide)]

    def along(step):
        return pltpu.make_async_remote_copy(
            src_ref=pick_out.at[lax.rem(row + step, tall)],
            dst_ref=pick_in.at[step],
            send_sem=pick_send.at[step],
            recv_sem=pick_recv.at[step],
            device_id=(lax.rem(row + step, tall) * wide + col, g),
            device_id_type=MESH,
        )

    for step in range(1, tall):
        along(step).start()
    pick_in[0] = pick_out[row]
    for step in range(1, wide):
        across(step).wait_send()
    for step in range(1, tall):
        along(step).wait_recv()
    final = pick_in[lax.rem(row - origin_row + tall, tall)]
    for span in range(spans):
        count = min(lanes, 7 * width - span * lanes)
        out[:, 0, pl.ds(span * lanes, count)] = final[span * rows : (span + 1) * rows, :count]

    for step in range(1, tall):
        along(step).wait_send()


def shards(deflation, operator_tiles, tile_columns, neighbours, send_blocks, row_owner):
    subs, grps = lax.axis_size("sub"), lax.axis_size("grp")
    wide = 1 << (subs.bit_length() // 2)
    tall = subs // wide
    _, blocks, width, lanes = deflation.shape
    nt = operator_tiles.shape[2]
    own_blocks = blocks * grps
    total_cols = own_blocks + 6 * SEND_COUNT
    spans = -(-7 * width // lanes)
    rows = width // grps
    packed = -(-spans * rows // 8) * 8
    bf16, f32, i32 = jnp.bfloat16, jnp.float32, jnp.int32
    dma = pltpu.SemaphoreType.DMA
    sizes = (subs, grps, wide, tall, blocks, width, nt)
    result = pl.pallas_call(
        functools.partial(kernel, sizes),
        out_shape=jax.ShapeDtypeStruct((rows, 1, 7 * width), f32),
        in_specs=[pl.BlockSpec(memory_space=pltpu.HBM)] * 6,
        out_specs=pl.BlockSpec(memory_space=pltpu.VMEM),
        scratch_shapes=[
            pltpu.VMEM((blocks, width, lanes), bf16),
            pltpu.VMEM((2, blocks // 2, width, lanes), bf16),
            pltpu.VMEM((own_blocks // 2, width, lanes), bf16),
            pltpu.VMEM((own_blocks, width, lanes), f32),
            pltpu.VMEM((blocks, nt, lanes, lanes), bf16),
            pltpu.VMEM((blocks * nt * width, lanes), f32),
            pltpu.VMEM((total_cols * width, lanes), f32),
            pltpu.VMEM((2, total_cols // 2, width, lanes), bf16),
            pltpu.VMEM((own_blocks // 2, width, lanes), bf16),
            pltpu.VMEM((3 * SEND_COUNT, width, lanes), bf16),
            pltpu.VMEM((3 * SEND_COUNT, width, lanes), bf16),
            pltpu.VMEM((6, SEND_COUNT // 2, width, lanes), bf16),
            pltpu.VMEM((6, SEND_COUNT // 2, width, lanes), bf16),
            pltpu.VMEM((6, width, width), f32),
            pltpu.VMEM((width, spans * lanes), f32),
            pltpu.VMEM((grps, packed, lanes), f32),
            pltpu.VMEM((grps, packed, lanes), f32),
            pltpu.VMEM((wide, packed, lanes), f32),
            pltpu.VMEM((tall, packed, lanes), f32),
            pltpu.VMEM((tall, packed, lanes), f32),
            pltpu.SMEM((blocks, 1, nt), i32),
            pltpu.SMEM((1, 6), i32),
            pltpu.SMEM((6, 1, SEND_COUNT), i32),
            pltpu.SMEM((subs,), i32),
            dma,
            dma((blocks,)),
            dma((4,)),
            dma((grps,)),
            dma((grps,)),
            dma((2,)),
            dma((2,)),
            dma((6,)),
            dma((6,)),
            dma((grps,)),
            dma((grps,)),
            dma((wide,)),
            dma((wide,)),
            dma((tall,)),
            dma((tall,)),
            pltpu.SemaphoreType.REGULAR((max(1, len(reaches_of(subs))),)),
        ],
        compiler_params=pltpu.CompilerParams(
            collective_id=0, has_side_effects=True, vmem_limit_bytes=40 * 2**20
        ),
    )(
        *(
            pltpu.with_memory_space_constraint(operand, pltpu.HBM)
            for operand in (
                deflation,
                operator_tiles,
                tile_columns.reshape(blocks, 1, nt),
                neighbours,
                send_blocks.reshape(6, 1, SEND_COUNT),
                row_owner,
            )
        )
    )
    return result.reshape(1, rows, 7 * width)


def solution(mesh):
    placed = (
        P("sub", "grp", None, None),
        P("sub", "grp", None, None, None),
        P("sub", "grp", None),
        P("sub", None),
        P("sub", None, None),
        P(),
    )
    return jax.shard_map(
        shards, mesh=mesh, in_specs=placed, out_specs=P("sub", "grp", None), check_vma=False
    )
```

```python
import functools

import jax
import jax.numpy as jnp
from jax import lax
from jax.experimental import pallas as pl
from jax.experimental.pallas import tpu as pltpu
from jax.sharding import PartitionSpec as P

OFFSETS = (1, 2, 3, -1, -2, -3)
ORDER = (2, 5, 1, 4, 0, 3)
SEND_COUNT = 8
MESH = pl.DeviceIdType.MESH


def reaches_of(subs):
    return [1 << level for level in range(1, max(1, subs.bit_length() - 2))]


def kernel(
    sizes,
    defl,
    tiles,
    cols,
    neigh,
    lists,
    owner,
    out,
    mine,
    split,
    half_panel,
    spread,
    op,
    y_buf,
    z_buf,
    z_split,
    z_own,
    z_margin,
    z_sum,
    send_buf,
    recv_buf,
    g_buf,
    g_full,
    part_out,
    part_in,
    row_in,
    pick_out,
    pick_in,
    s_cols,
    s_neigh,
    s_lists,
    s_owner,
    load_sem,
    op_sem,
    table_sem,
    panel_send,
    panel_recv,
    z_send,
    z_recv,
    margin_send,
    margin_recv,
    part_send,
    part_recv,
    row_send,
    row_recv,
    pick_send,
    pick_recv,
    greet_sem,
):
    subs, grps, wide, tall, blocks, width, nt = sizes
    lanes = 128
    own_blocks = blocks * grps
    total_cols = own_blocks + 6 * SEND_COUNT
    n_tiles = blocks * nt
    reaches = reaches_of(subs)
    rows = width // grps
    pairs = blocks // 2
    own_pairs = own_blocks // 2
    margin_pairs = SEND_COUNT // 2

    i = lax.axis_index("sub")
    g = lax.axis_index("grp")
    row, col = i // wide, i % wide
    parity = lax.rem(g, 2)

    def grp_peer(step):
        return lax.rem(g + step + grps, grps)

    def sub_peer(step):
        return lax.rem(i + step + subs, subs)

    def greet(level):
        if level < len(reaches):
            for step in (reaches[level], -reaches[level]):
                pl.semaphore_signal(
                    greet_sem.at[level], inc=1, device_id=(sub_peer(step), g), device_id_type=MESH
                )

    def greeted(level):
        if level < len(reaches):
            pl.semaphore_wait(greet_sem.at[level], 2)

    op_copies = [
        pltpu.make_async_copy(tiles.at[0, b], op.at[b], op_sem.at[b]) for b in range(blocks)
    ]
    table_copies = [
        pltpu.make_async_copy(cols, s_cols, table_sem.at[0]),
        pltpu.make_async_copy(neigh, s_neigh, table_sem.at[1]),
        pltpu.make_async_copy(lists, s_lists, table_sem.at[2]),
        pltpu.make_async_copy(owner, s_owner, table_sem.at[3]),
    ]
    own_copy = pltpu.make_async_copy(defl.at[0], mine, load_sem)
    own_copy.start()

    low_lanes = lax.broadcasted_iota(jnp.int32, (width, lanes), 1) < lanes // 2

    def halves(first, second):
        turned_first = pltpu.roll(first, lanes // 2, 1)
        turned_second = pltpu.roll(second, lanes // 2, 1)
        low = jnp.where(low_lanes, first, turned_second)
        high = jnp.where(low_lanes, turned_first, second)
        return low.astype(jnp.bfloat16), high.astype(jnp.bfloat16)

    barrier = pltpu.get_barrier_semaphore()
    for step in range(1, grps):
        pl.semaphore_signal(barrier, inc=1, device_id=(i, grp_peer(step)), device_id_type=MESH)
    for step in (1, -1, 2, -2):
        pl.semaphore_signal(barrier, inc=1, device_id=(sub_peer(step), g), device_id_type=MESH)
    own_copy.wait()
    for p in range(pairs):
        first, second = mine[2 * p].astype(jnp.float32), mine[2 * p + 1].astype(jnp.float32)
        split[0, p], split[1, p] = halves(first, second)
    pl.semaphore_wait(barrier, grps + 3)

    def panel_copy(step):
        return pltpu.make_async_remote_copy(
            src_ref=split.at[lax.rem(g + step, 2)],
            dst_ref=half_panel.at[pl.ds(g * pairs, pairs)],
            send_sem=panel_send.at[step],
            recv_sem=panel_recv.at[step],
            device_id=(i, grp_peer(step)),
            device_id_type=MESH,
        )

    def panel_arrival(step):
        place = half_panel.at[pl.ds(grp_peer(-step) * pairs, pairs)]
        return pltpu.make_async_remote_copy(
            src_ref=place,
            dst_ref=place,
            send_sem=panel_send.at[step],
            recv_sem=panel_recv.at[step],
            device_id=(i, grp_peer(step)),
            device_id_type=MESH,
        )

    near_first = sorted(range(1, grps), key=lambda s: min(s, grps - s))
    for step in near_first:
        panel_copy(step).start()
    greet(0)
    for copy in op_copies + table_copies:
        copy.start()

    def products(b):
        op_copies[b].wait()
        left = mine[b]
        for t in range(nt):
            y_buf[pl.ds((b * nt + t) * width, width), :] = jnp.dot(
                left, op[b, t], preferred_element_type=jnp.float32
            )

    def by_column(first, last, picker):
        for a in range(first, last):
            by_tile = y_buf[pl.ds(a, n_tiles, stride=width), :].astype(jnp.bfloat16)
            z_buf[pl.ds(a, total_cols, stride=width), :] = jnp.dot(
                picker, by_tile, preferred_element_type=jnp.float32
            )

    for b in range(blocks):
        products(b)
    greeted(0)
    greet(1)
    for copy in table_copies:
        copy.wait()
    lane_of = lax.broadcasted_iota(jnp.int32, (8, lanes), 1)
    named = jnp.full((8, lanes), -1, jnp.int32)
    for b in range(blocks):
        for t in range(nt):
            named = jnp.where(lane_of == b * nt + t, s_cols[b, 0, t], named)
    moved = named
    for r in range(6):
        low = own_blocks + r * SEND_COUNT
        within = (named >= low) & (named < low + SEND_COUNT)
        moved = moved + jnp.where(within, (s_neigh[0, r] - r) * SEND_COUNT, 0)
    named = jnp.broadcast_to(moved[0:1, :], (total_cols, lanes))
    hits = lax.broadcasted_iota(jnp.int32, (total_cols, lanes), 0) == named
    picker = jnp.where(hits, 1.0, 0.0).astype(jnp.bfloat16)[:, :n_tiles]
    by_column(0, width, picker)
    for p in range(total_cols // 2):
        first = z_buf[pl.ds(2 * p * width, width), :]
        second = z_buf[pl.ds((2 * p + 1) * width, width), :]
        z_split[0, p], z_split[1, p] = halves(first, second)

    def z_copy(which):
        first, count = (0, own_pairs) if which == 0 else (own_pairs, 6 * margin_pairs)
        return pltpu.make_async_remote_copy(
            src_ref=z_split.at[1 - parity, pl.ds(first, count)],
            dst_ref=(z_own, z_margin)[which],
            send_sem=z_send.at[which],
            recv_sem=z_recv.at[which],
            device_id=(i, grp_peer(2 * which - 1)),
            device_id_type=MESH,
        )

    z_copy(0).start()
    z_copy(1).start()
    greeted(1)
    greet(2)

    def spread_blocks(origin):
        for p in range(pairs):
            packed = half_panel[origin * pairs + p].astype(jnp.float32)
            turned = pltpu.roll(packed, lanes // 2, 1)
            spread[origin * blocks + 2 * p] = jnp.where(low_lanes, packed, turned)
            spread[origin * blocks + 2 * p + 1] = jnp.where(low_lanes, turned, packed)

    for p in range(pairs):
        half_panel[g * pairs + p] = split[parity, p]
    spread_blocks(g)
    for step in near_first:
        panel_arrival(step).wait_recv()
        spread_blocks(grp_peer(-step))

    def margin(o):
        there = i - OFFSETS[o]
        return pltpu.make_async_remote_copy(
            src_ref=send_buf.at[o],
            dst_ref=recv_buf.at[o],
            send_sem=margin_send.at[o],
            recv_sem=margin_recv.at[o],
            device_id=(there, g),
            device_id_type=MESH,
        )

    def inside(there):
        return (there >= 0) & (there < subs)

    greeted(2)
    greet(3)
    for o in ORDER:
        for p in range(margin_pairs):
            first, second = spread[s_lists[o, 0, 2 * p]], spread[s_lists[o, 0, 2 * p + 1]]
            send_buf[o, p] = jnp.where(low_lanes, first, second).astype(jnp.bfloat16)

        @pl.when(inside(i - OFFSETS[o]))
        def _():
            margin(o).start()

    def contract(left, right):
        return lax.dot_general(
            jnp.concatenate(left, axis=1),
            jnp.concatenate(right, axis=1),
            (((1,), (1,)), ((), ())),
            preferred_element_type=jnp.float32,
        )

    for o in range(6):

        @pl.when(jnp.logical_not(inside(i + OFFSETS[o])))
        def _():
            recv_buf[o] = jnp.zeros_like(recv_buf[o])

    part_out[...] = jnp.zeros_like(part_out)
    g_full[...] = jnp.zeros_like(g_full)
    chosen = []
    for target in range(tall):
        place = jnp.int32(0)
        for c in range(1, wide):
            place = jnp.where(s_owner[row * wide + c] == target * wide + col, c, place)
        chosen.append(place)
    origin_row = jnp.int32(0)
    for s in range(subs):
        origin_row = jnp.where(s_owner[s] == i, s // wide, origin_row)

    def both(theirs, p, q):
        total = z_split[parity, p].astype(jnp.float32) + theirs[q].astype(jnp.float32)
        return total.astype(jnp.bfloat16)

    z_copy(0).wait_recv()
    own = jnp.zeros((width, width), jnp.float32)
    for origin in range(grps):
        places = range(origin * pairs, (origin + 1) * pairs)
        own = own + contract([both(z_own, p, p) for p in places], [half_panel[p] for p in places])
    g_full[:, pl.ds(0, width)] = own
    z_copy(1).wait_recv()
    for p in range(6 * margin_pairs):
        z_sum[p] = both(z_margin, own_pairs + p, p)

    for o in ORDER:

        @pl.when(inside(i + OFFSETS[o]))
        def _():
            margin(o).wait_recv()

    places = range(margin_pairs)
    for o in range(6):
        g_buf[o] = contract(
            [z_sum[o * margin_pairs + p] for p in places], [recv_buf[o, p] for p in places]
        )

    for r in range(6):
        slot = s_neigh[0, r]
        value = g_buf[jnp.maximum(slot, 0)]
        g_full[:, pl.ds((r + 1) * width, width)] = jnp.where(
            jnp.full((width, width), slot) >= 0, value, 0.0
        )

    spans = -(-7 * width // lanes)
    for other in range(grps):
        for span in range(spans):
            part_out[other, pl.ds(span * rows, rows), :] = g_full[
                pl.ds(other * rows, rows), pl.ds(span * lanes, lanes)
            ]

    greeted(3)

    def part(step):
        return pltpu.make_async_remote_copy(
            src_ref=part_out.at[grp_peer(step)],
            dst_ref=part_in.at[step],
            send_sem=part_send.at[step],
            recv_sem=part_recv.at[step],
            device_id=(i, grp_peer(step)),
            device_id_type=MESH,
        )

    for step in reversed(near_first):
        part(step).start()
    for step in range(1, grps):
        panel_copy(step).wait_send()
    z_copy(0).wait_send()
    z_copy(1).wait_send()
    for o in ORDER:

        @pl.when(inside(i - OFFSETS[o]))
        def _():
            margin(o).wait_send()

    summed = part_out[g]
    for step in near_first:
        part(step).wait_recv()
        summed = summed + part_in[step]

    row_in[0] = summed

    def across(step):
        return pltpu.make_async_remote_copy(
            src_ref=row_in.at[0],
            dst_ref=row_in.at[step],
            send_sem=row_send.at[step],
            recv_sem=row_recv.at[step],
            device_id=(row * wide + lax.rem(col + step, wide), g),
            device_id_type=MESH,
        )

    for step in sorted(range(1, wide), key=lambda s: -min(s, wide - s)):
        across(step).start()
    for step in range(1, grps):
        part(step).wait_send()
    for step in range(1, wide):
        across(step).wait_recv()
    for target in range(tall):
        pick_out[target] = row_in[lax.rem(col - chosen[target] + wide, wide)]

    def along(step):
        return pltpu.make_async_remote_copy(
            src_ref=pick_out.at[lax.rem(row + step, tall)],
            dst_ref=pick_in.at[step],
            send_sem=pick_send.at[step],
            recv_sem=pick_recv.at[step],
            device_id=(lax.rem(row + step, tall) * wide + col, g),
            device_id_type=MESH,
        )

    for step in sorted(range(1, tall), key=lambda s: -min(s, tall - s)):
        along(step).start()
    pick_in[0] = pick_out[row]
    for step in range(1, wide):
        across(step).wait_send()
    for step in range(1, tall):
        along(step).wait_recv()
    final = pick_in[lax.rem(row - origin_row + tall, tall)]
    for span in range(spans):
        count = min(lanes, 7 * width - span * lanes)
        out[:, 0, pl.ds(span * lanes, count)] = final[span * rows : (span + 1) * rows, :count]

    for step in range(1, tall):
        along(step).wait_send()


def shards(deflation, operator_tiles, tile_columns, neighbours, send_blocks, row_owner):
    subs, grps = lax.axis_size("sub"), lax.axis_size("grp")
    wide = 1 << (subs.bit_length() // 2)
    tall = subs // wide
    _, blocks, width, lanes = deflation.shape
    nt = operator_tiles.shape[2]
    own_blocks = blocks * grps
    total_cols = own_blocks + 6 * SEND_COUNT
    spans = -(-7 * width // lanes)
    rows = width // grps
    packed = -(-spans * rows // 8) * 8
    bf16, f32, i32 = jnp.bfloat16, jnp.float32, jnp.int32
    dma = pltpu.SemaphoreType.DMA
    sizes = (subs, grps, wide, tall, blocks, width, nt)
    result = pl.pallas_call(
        functools.partial(kernel, sizes),
        out_shape=jax.ShapeDtypeStruct((rows, 1, 7 * width), f32),
        in_specs=[pl.BlockSpec(memory_space=pltpu.HBM)] * 6,
        out_specs=pl.BlockSpec(memory_space=pltpu.VMEM),
        scratch_shapes=[
            pltpu.VMEM((blocks, width, lanes), bf16),
            pltpu.VMEM((2, blocks // 2, width, lanes), bf16),
            pltpu.VMEM((own_blocks // 2, width, lanes), bf16),
            pltpu.VMEM((own_blocks, width, lanes), f32),
            pltpu.VMEM((blocks, nt, lanes, lanes), bf16),
            pltpu.VMEM((blocks * nt * width, lanes), f32),
            pltpu.VMEM((total_cols * width, lanes), f32),
            pltpu.VMEM((2, total_cols // 2, width, lanes), bf16),
            pltpu.VMEM((own_blocks // 2, width, lanes), bf16),
            pltpu.VMEM((3 * SEND_COUNT, width, lanes), bf16),
            pltpu.VMEM((3 * SEND_COUNT, width, lanes), bf16),
            pltpu.VMEM((6, SEND_COUNT // 2, width, lanes), bf16),
            pltpu.VMEM((6, SEND_COUNT // 2, width, lanes), bf16),
            pltpu.VMEM((6, width, width), f32),
            pltpu.VMEM((width, spans * lanes), f32),
            pltpu.VMEM((grps, packed, lanes), f32),
            pltpu.VMEM((grps, packed, lanes), f32),
            pltpu.VMEM((wide, packed, lanes), f32),
            pltpu.VMEM((tall, packed, lanes), f32),
            pltpu.VMEM((tall, packed, lanes), f32),
            pltpu.SMEM((blocks, 1, nt), i32),
            pltpu.SMEM((1, 6), i32),
            pltpu.SMEM((6, 1, SEND_COUNT), i32),
            pltpu.SMEM((subs,), i32),
            dma,
            dma((blocks,)),
            dma((4,)),
            dma((grps,)),
            dma((grps,)),
            dma((2,)),
            dma((2,)),
            dma((6,)),
            dma((6,)),
            dma((grps,)),
            dma((grps,)),
            dma((wide,)),
            dma((wide,)),
            dma((tall,)),
            dma((tall,)),
            pltpu.SemaphoreType.REGULAR((max(1, len(reaches_of(subs))),)),
        ],
        compiler_params=pltpu.CompilerParams(
            collective_id=0, has_side_effects=True, vmem_limit_bytes=40 * 2**20
        ),
    )(
        *(
            pltpu.with_memory_space_constraint(operand, pltpu.HBM)
            for operand in (
                deflation,
                operator_tiles,
                tile_columns.reshape(blocks, 1, nt),
                neighbours,
                send_blocks.reshape(6, 1, SEND_COUNT),
                row_owner,
            )
        )
    )
    return result.reshape(1, rows, 7 * width)


def solution(mesh):
    placed = (
        P("sub", "grp", None, None),
        P("sub", "grp", None, None, None),
        P("sub", "grp", None),
        P("sub", None),
        P("sub", None, None),
        P(),
    )
    return jax.shard_map(
        shards, mesh=mesh, in_specs=placed, out_specs=P("sub", "grp", None), check_vma=False
    )
```

```python
import functools

import jax
import jax.numpy as jnp
from jax import lax
from jax.experimental import pallas as pl
from jax.experimental.pallas import tpu as pltpu
from jax.sharding import PartitionSpec as P

OFFSETS = (1, 2, 3, -1, -2, -3)
ORDER = (2, 5, 1, 4, 0, 3)
SEND_COUNT = 8
MESH = pl.DeviceIdType.MESH


def reaches_of(subs):
    return [1 << level for level in range(1, max(1, subs.bit_length() - 2))]


def kernel(
    sizes,
    defl,
    tiles,
    cols,
    neigh,
    lists,
    owner,
    out,
    mine,
    split,
    half_panel,
    spread,
    op,
    y_buf,
    z_buf,
    z_split,
    z_own,
    z_margin,
    z_sum,
    send_buf,
    recv_buf,
    g_buf,
    g_full,
    part_out,
    part_in,
    row_in,
    pick_out,
    pick_in,
    s_cols,
    s_neigh,
    s_lists,
    s_owner,
    load_sem,
    op_sem,
    table_sem,
    panel_send,
    panel_recv,
    z_send,
    z_recv,
    margin_send,
    margin_recv,
    part_send,
    part_recv,
    row_send,
    row_recv,
    pick_send,
    pick_recv,
    greet_sem,
):
    subs, grps, wide, tall, blocks, width, nt = sizes
    lanes = 128
    own_blocks = blocks * grps
    total_cols = own_blocks + 6 * SEND_COUNT
    n_tiles = blocks * nt
    reaches = reaches_of(subs)
    rows = width // grps
    pairs = blocks // 2
    own_pairs = own_blocks // 2
    margin_pairs = SEND_COUNT // 2

    i = lax.axis_index("sub")
    g = lax.axis_index("grp")
    row, col = i // wide, i % wide
    parity = lax.rem(g, 2)

    def grp_peer(step):
        return lax.rem(g + step + grps, grps)

    def sub_peer(step):
        return lax.rem(i + step + subs, subs)

    def greet(level):
        if level < len(reaches):
            for step in (reaches[level], -reaches[level]):
                pl.semaphore_signal(
                    greet_sem.at[level], inc=1, device_id=(sub_peer(step), g), device_id_type=MESH
                )

    def greeted(level):
        if level < len(reaches):
            pl.semaphore_wait(greet_sem.at[level], 2)

    op_copies = [
        pltpu.make_async_copy(tiles.at[0, b], op.at[b], op_sem.at[b]) for b in range(blocks)
    ]
    table_copies = [
        pltpu.make_async_copy(cols, s_cols, table_sem.at[0]),
        pltpu.make_async_copy(neigh, s_neigh, table_sem.at[1]),
        pltpu.make_async_copy(lists, s_lists, table_sem.at[2]),
        pltpu.make_async_copy(owner, s_owner, table_sem.at[3]),
    ]
    own_copy = pltpu.make_async_copy(defl.at[0], mine, load_sem)
    own_copy.start()

    low_lanes = lax.broadcasted_iota(jnp.int32, (width, lanes), 1) < lanes // 2

    def halves(first, second):
        turned_first = pltpu.roll(first, lanes // 2, 1)
        turned_second = pltpu.roll(second, lanes // 2, 1)
        low = jnp.where(low_lanes, first, turned_second)
        high = jnp.where(low_lanes, turned_first, second)
        return low.astype(jnp.bfloat16), high.astype(jnp.bfloat16)

    barrier = pltpu.get_barrier_semaphore()
    for step in range(1, grps):
        pl.semaphore_signal(barrier, inc=1, device_id=(i, grp_peer(step)), device_id_type=MESH)
    for step in (1, -1, 2, -2):
        pl.semaphore_signal(barrier, inc=1, device_id=(sub_peer(step), g), device_id_type=MESH)
    own_copy.wait()
    for p in range(pairs):
        first, second = mine[2 * p].astype(jnp.float32), mine[2 * p + 1].astype(jnp.float32)
        split[0, p], split[1, p] = halves(first, second)
    pl.semaphore_wait(barrier, grps + 3)

    def panel_copy(step):
        return pltpu.make_async_remote_copy(
            src_ref=split.at[lax.rem(g + step, 2)],
            dst_ref=half_panel.at[pl.ds(g * pairs, pairs)],
            send_sem=panel_send.at[step],
            recv_sem=panel_recv.at[step],
            device_id=(i, grp_peer(step)),
            device_id_type=MESH,
        )

    def panel_arrival(step):
        place = half_panel.at[pl.ds(grp_peer(-step) * pairs, pairs)]
        return pltpu.make_async_remote_copy(
            src_ref=place,
            dst_ref=place,
            send_sem=panel_send.at[step],
            recv_sem=panel_recv.at[step],
            device_id=(i, grp_peer(step)),
            device_id_type=MESH,
        )

    near_first = sorted(range(1, grps), key=lambda s: min(s, grps - s))
    for step in near_first:
        panel_copy(step).start()
    greet(0)
    for copy in op_copies + table_copies:
        copy.start()

    def products(b):
        op_copies[b].wait()
        left = mine[b]
        for t in range(nt):
            y_buf[pl.ds((b * nt + t) * width, width), :] = jnp.dot(
                left, op[b, t], preferred_element_type=jnp.float32
            )

    def by_column(first, last, picker):
        for a in range(first, last):
            by_tile = y_buf[pl.ds(a, n_tiles, stride=width), :].astype(jnp.bfloat16)
            z_buf[pl.ds(a, total_cols, stride=width), :] = jnp.dot(
                picker, by_tile, preferred_element_type=jnp.float32
            )

    for b in range(blocks):
        products(b)
    greeted(0)
    greet(1)
    for copy in table_copies:
        copy.wait()
    lane_of = lax.broadcasted_iota(jnp.int32, (8, lanes), 1)
    named = jnp.full((8, lanes), -1, jnp.int32)
    for b in range(blocks):
        for t in range(nt):
            named = jnp.where(lane_of == b * nt + t, s_cols[b, 0, t], named)
    moved = named
    for r in range(6):
        low = own_blocks + r * SEND_COUNT
        within = (named >= low) & (named < low + SEND_COUNT)
        moved = moved + jnp.where(within, (s_neigh[0, r] - r) * SEND_COUNT, 0)
    named = jnp.broadcast_to(moved[0:1, :], (total_cols, lanes))
    hits = lax.broadcasted_iota(jnp.int32, (total_cols, lanes), 0) == named
    picker = jnp.where(hits, 1.0, 0.0).astype(jnp.bfloat16)[:, :n_tiles]
    by_column(0, width, picker)
    for p in range(total_cols // 2):
        first = z_buf[pl.ds(2 * p * width, width), :]
        second = z_buf[pl.ds((2 * p + 1) * width, width), :]
        z_split[0, p], z_split[1, p] = halves(first, second)

    def z_copy(which):
        first, count = (0, own_pairs) if which == 0 else (own_pairs, 6 * margin_pairs)
        return pltpu.make_async_remote_copy(
            src_ref=z_split.at[1 - parity, pl.ds(first, count)],
            dst_ref=(z_own, z_margin)[which],
            send_sem=z_send.at[which],
            recv_sem=z_recv.at[which],
            device_id=(i, grp_peer(2 * which - 1)),
            device_id_type=MESH,
        )

    z_copy(0).start()
    z_copy(1).start()
    greeted(1)
    greet(2)

    def spread_blocks(origin):
        for p in range(pairs):
            packed = half_panel[origin * pairs + p].astype(jnp.float32)
            turned = pltpu.roll(packed, lanes // 2, 1)
            spread[origin * blocks + 2 * p] = jnp.where(low_lanes, packed, turned)
            spread[origin * blocks + 2 * p + 1] = jnp.where(low_lanes, turned, packed)

    for p in range(pairs):
        half_panel[g * pairs + p] = split[parity, p]
    spread_blocks(g)
    for step in near_first:
        panel_arrival(step).wait_recv()
        spread_blocks(grp_peer(-step))

    def margin(o):
        there = i - OFFSETS[o]
        return pltpu.make_async_remote_copy(
            src_ref=send_buf.at[o],
            dst_ref=recv_buf.at[o],
            send_sem=margin_send.at[o],
            recv_sem=margin_recv.at[o],
            device_id=(there, g),
            device_id_type=MESH,
        )

    def inside(there):
        return (there >= 0) & (there < subs)

    greeted(2)
    greet(3)
    for o in ORDER:
        for p in range(margin_pairs):
            first, second = spread[s_lists[o, 0, 2 * p]], spread[s_lists[o, 0, 2 * p + 1]]
            send_buf[o, p] = jnp.where(low_lanes, first, second).astype(jnp.bfloat16)

        @pl.when(inside(i - OFFSETS[o]))
        def _():
            margin(o).start()

    def contract(left, right):
        return lax.dot_general(
            jnp.concatenate(left, axis=1),
            jnp.concatenate(right, axis=1),
            (((1,), (1,)), ((), ())),
            preferred_element_type=jnp.float32,
        )

    for o in range(6):

        @pl.when(jnp.logical_not(inside(i + OFFSETS[o])))
        def _():
            recv_buf[o] = jnp.zeros_like(recv_buf[o])

    part_out[...] = jnp.zeros_like(part_out)
    g_full[...] = jnp.zeros_like(g_full)
    chosen = []
    for target in range(tall):
        place = jnp.int32(0)
        for c in range(1, wide):
            place = jnp.where(s_owner[row * wide + c] == target * wide + col, c, place)
        chosen.append(place)
    origin_row = jnp.int32(0)
    for s in range(subs):
        origin_row = jnp.where(s_owner[s] == i, s // wide, origin_row)

    def both(theirs, p, q):
        total = z_split[parity, p].astype(jnp.float32) + theirs[q].astype(jnp.float32)
        return total.astype(jnp.bfloat16)

    z_copy(0).wait_recv()
    own = jnp.zeros((width, width), jnp.float32)
    for origin in range(grps):
        places = range(origin * pairs, (origin + 1) * pairs)
        own = own + contract([both(z_own, p, p) for p in places], [half_panel[p] for p in places])
    g_full[pl.ds(0, width), pl.ds(0, width)] = own
    z_copy(1).wait_recv()
    for p in range(6 * margin_pairs):
        z_sum[p] = both(z_margin, own_pairs + p, p)

    for o in ORDER:

        @pl.when(inside(i + OFFSETS[o]))
        def _():
            margin(o).wait_recv()

    places = range(margin_pairs)
    for o in range(6):
        g_buf[o] = contract(
            [z_sum[o * margin_pairs + p] for p in places], [recv_buf[o, p] for p in places]
        )

    for r in range(6):
        slot = s_neigh[0, r]
        value = g_buf[jnp.maximum(slot, 0)]
        g_full[pl.ds(0, width), pl.ds((r + 1) * width, width)] = jnp.where(
            jnp.full((width, width), slot) >= 0, value, 0.0
        )

    spans = -(-7 * width // lanes)
    packed = part_in.shape[1]
    for other in range(grps):
        for span in range(spans):
            part_out[other, pl.ds(span * rows, rows), :] = g_full[
                pl.ds(other * rows, rows), pl.ds(span * lanes, lanes)
            ]

    greeted(3)

    def part(step):
        return pltpu.make_async_remote_copy(
            src_ref=part_out.at[grp_peer(step), pl.ds(0, packed)],
            dst_ref=part_in.at[step],
            send_sem=part_send.at[step],
            recv_sem=part_recv.at[step],
            device_id=(i, grp_peer(step)),
            device_id_type=MESH,
        )

    for step in reversed(near_first):
        part(step).start()
    for step in range(1, grps):
        panel_copy(step).wait_send()
    z_copy(0).wait_send()
    z_copy(1).wait_send()
    for o in ORDER:

        @pl.when(inside(i - OFFSETS[o]))
        def _():
            margin(o).wait_send()

    summed = part_out[g, pl.ds(0, packed)]
    for step in near_first:
        part(step).wait_recv()
        summed = summed + part_in[step]

    row_in[0] = summed

    def across(step):
        return pltpu.make_async_remote_copy(
            src_ref=row_in.at[0],
            dst_ref=row_in.at[step],
            send_sem=row_send.at[step],
            recv_sem=row_recv.at[step],
            device_id=(row * wide + lax.rem(col + step, wide), g),
            device_id_type=MESH,
        )

    for step in sorted(range(1, wide), key=lambda s: -min(s, wide - s)):
        across(step).start()
    for step in range(1, grps):
        part(step).wait_send()
    for step in range(1, wide):
        across(step).wait_recv()
    for target in range(tall):
        pick_out[target] = row_in[lax.rem(col - chosen[target] + wide, wide)]

    def along(step):
        return pltpu.make_async_remote_copy(
            src_ref=pick_out.at[lax.rem(row + step, tall)],
            dst_ref=pick_in.at[step],
            send_sem=pick_send.at[step],
            recv_sem=pick_recv.at[step],
            device_id=(lax.rem(row + step, tall) * wide + col, g),
            device_id_type=MESH,
        )

    for step in sorted(range(1, tall), key=lambda s: -min(s, tall - s)):
        along(step).start()
    pick_in[0] = pick_out[row]
    for step in range(1, wide):
        across(step).wait_send()
    for step in range(1, tall):
        along(step).wait_recv()
    final = pick_in[lax.rem(row - origin_row + tall, tall)]
    for span in range(spans):
        count = min(lanes, 7 * width - span * lanes)
        out[:, 0, pl.ds(span * lanes, count)] = final[span * rows : (span + 1) * rows, :count]

    for step in range(1, tall):
        along(step).wait_send()


def shards(deflation, operator_tiles, tile_columns, neighbours, send_blocks, row_owner):
    subs, grps = lax.axis_size("sub"), lax.axis_size("grp")
    wide = 1 << (subs.bit_length() // 2)
    tall = subs // wide
    _, blocks, width, lanes = deflation.shape
    nt = operator_tiles.shape[2]
    own_blocks = blocks * grps
    total_cols = own_blocks + 6 * SEND_COUNT
    spans = -(-7 * width // lanes)
    rows = width // grps
    packed = -(-spans * rows // 8) * 8
    bf16, f32, i32 = jnp.bfloat16, jnp.float32, jnp.int32
    dma = pltpu.SemaphoreType.DMA
    sizes = (subs, grps, wide, tall, blocks, width, nt)
    result = pl.pallas_call(
        functools.partial(kernel, sizes),
        out_shape=jax.ShapeDtypeStruct((rows, 1, 7 * width), f32),
        in_specs=[pl.BlockSpec(memory_space=pltpu.HBM)] * 6,
        out_specs=pl.BlockSpec(memory_space=pltpu.VMEM),
        scratch_shapes=[
            pltpu.VMEM((blocks, width, lanes), bf16),
            pltpu.VMEM((2, blocks // 2, width, lanes), bf16),
            pltpu.VMEM((own_blocks // 2, width, lanes), bf16),
            pltpu.VMEM((own_blocks, width, lanes), f32),
            pltpu.VMEM((blocks, nt, lanes, lanes), bf16),
            pltpu.VMEM(((blocks * nt + 8) * width, lanes), f32),
            pltpu.VMEM(((total_cols + 8) * width, lanes), f32),
            pltpu.VMEM((2, total_cols // 2, width, lanes), bf16),
            pltpu.VMEM((own_blocks // 2, width, lanes), bf16),
            pltpu.VMEM((3 * SEND_COUNT, width, lanes), bf16),
            pltpu.VMEM((3 * SEND_COUNT, width, lanes), bf16),
            pltpu.VMEM((6, SEND_COUNT // 2, width, lanes), bf16),
            pltpu.VMEM((6, SEND_COUNT // 2, width, lanes), bf16),
            pltpu.VMEM((6, width, width), f32),
            pltpu.VMEM((width + 8, spans * lanes), f32),
            pltpu.VMEM((grps, packed + 8, lanes), f32),
            pltpu.VMEM((grps, packed, lanes), f32),
            pltpu.VMEM((wide, packed, lanes), f32),
            pltpu.VMEM((tall, packed, lanes), f32),
            pltpu.VMEM((tall, packed, lanes), f32),
            pltpu.SMEM((blocks, 1, nt), i32),
            pltpu.SMEM((1, 6), i32),
            pltpu.SMEM((6, 1, SEND_COUNT), i32),
            pltpu.SMEM((subs,), i32),
            dma,
            dma((blocks,)),
            dma((4,)),
            dma((grps,)),
            dma((grps,)),
            dma((2,)),
            dma((2,)),
            dma((6,)),
            dma((6,)),
            dma((grps,)),
            dma((grps,)),
            dma((wide,)),
            dma((wide,)),
            dma((tall,)),
            dma((tall,)),
            pltpu.SemaphoreType.REGULAR((max(1, len(reaches_of(subs))),)),
        ],
        compiler_params=pltpu.CompilerParams(
            collective_id=0, has_side_effects=True, vmem_limit_bytes=40 * 2**20
        ),
    )(
        *(
            pltpu.with_memory_space_constraint(operand, pltpu.HBM)
            for operand in (
                deflation,
                operator_tiles,
                tile_columns.reshape(blocks, 1, nt),
                neighbours,
                send_blocks.reshape(6, 1, SEND_COUNT),
                row_owner,
            )
        )
    )
    return result.reshape(1, rows, 7 * width)


def solution(mesh):
    placed = (
        P("sub", "grp", None, None),
        P("sub", "grp", None, None, None),
        P("sub", "grp", None),
        P("sub", None),
        P("sub", None, None),
        P(),
    )
    return jax.shard_map(
        shards, mesh=mesh, in_specs=placed, out_specs=P("sub", "grp", None), check_vma=False
    )
```
